32 devices in a mesh: ctx: 4 (over z), head: 4 (over y, x), dp: 2 (over core).
Axes of the slice: x: 2, y: 2, z: 4, core: 2. Of those that a mesh axis runs over, the one named last changes fastest.
Arguments:
- query_raw: bfloat16 [4096, 2048], P(('dp', 'ctx', 'head')), parts along dimension 0, may hold values from -6 to 6
- key_raw: bfloat16 [4096, 2048], P(('dp', 'ctx', 'head')), parts along dimension 0, may hold values from -6 to 6
- value_raw: bfloat16 [4096, 2048], P(('dp', 'ctx', 'head')), parts along dimension 0, may hold values from -6 to 6
- log_decay: bfloat16 [4096, 2048], P(('dp', 'ctx', 'head')), parts along dimension 0, may hold values from -1 to 0, as said below
- beta: bfloat16 [4096, 16], P(('dp', 'ctx', 'head')), parts along dimension 0, may hold values from 0.0029 to 1
- conv_weight: float32 [3, 4, 2048], replicated, may hold values from -3 to 3
- out_gate: bfloat16 [4096, 2048], P(('dp', 'ctx', 'head')), parts along dimension 0, may hold values from -6 to 6
- norm_gain: float32 [128], replicated, may hold values from 0.1 to 1.9
Outputs:
- mixed: bfloat16 [4096, 2048], P(('dp', 'ctx', 'head')), parts along dimension 0
The draws below stay inside these ranges and needn't reach their ends.
There are 2 independent parts, one for each index of `dp`. The reference program is written for one: setup_inputs(seed, part) draws one part's arguments, and reference() takes and returns one part's arrays. A program takes and returns all parts, laid end to end along the dimension named above; an argument that names none is the same for every part. Nothing has to cross between parts.
Inputs may be any that keep to these rules, and one draw needn't show every extreme that they name: `log_decay`: logarithms (all <= 0) of the decay factors of the state.
All inputs are finite; a program needn't handle non-finite values.
Results may differ from the reference program's by a relative error of at most 0.013.
Values may be sent and summed in bfloat16 or wider, within the bound.
No kernel may reach another device: no remote copies, remote signals or barrier semaphores. Data moves between devices by JAX's collectives and lax.ppermute only.
A program may use at most 64 MiB of HBM per device.

```python
import jax
import jax.numpy as jnp
from jax import lax

HEAD_COUNT = 16
HEAD_WIDTH = 128
CONV = 4
STRETCH = 64
HD = 2048
SPAN = 512
TOKEN_COUNT = 2048


def head_order(key):
    return jax.random.permutation(jax.random.fold_in(key, 101), HEAD_COUNT)


def draw_key_raw(key, part):
    input_flows = jax.random.split(jax.random.fold_in(key, 404), 3)
    magnitude = jax.random.uniform(input_flows[0], (1, HEAD_COUNT * HEAD_WIDTH), jnp.float32, 1.0, 2.5)
    sign_pick = jax.random.randint(input_flows[1], (1, HEAD_COUNT * HEAD_WIDTH), 0, 2).astype(jnp.float32) * 2.0 - 1.0
    jitter = jax.random.normal(input_flows[2], (TOKEN_COUNT, HEAD_COUNT * HEAD_WIDTH), jnp.float32)
    final_output = jnp.clip(magnitude * sign_pick + jitter, -6.0, 6.0)
    return final_output.astype(jnp.bfloat16)


def draw_beta(key, part):
    order = head_order(key)
    stride = 2
    strong_heads = order % stride == 0
    input_flows = jax.random.split(jax.random.fold_in(key, 202), 2)
    strong_draw = jnp.exp(jax.random.uniform(input_flows[0], (TOKEN_COUNT, HEAD_COUNT), jnp.float32, jnp.log(0.05), jnp.log(1.0)))
    weak_draw = jnp.exp(jax.random.uniform(input_flows[1], (TOKEN_COUNT, HEAD_COUNT), jnp.float32, jnp.log(0.003), jnp.log(0.03)))
    final_output = jnp.where(strong_heads[None, :], strong_draw, weak_draw)
    return final_output.astype(jnp.bfloat16)


def draw_log_decay(key, part):
    input_flows = jax.random.split(jax.random.fold_in(key, 303), 8)
    order = head_order(key)
    fast_count = HEAD_COUNT // 2
    rough_low = 0.5
    rough_high = 1.5
    fast_heads = order < fast_count
    fast_rate = 1.0 / jax.random.uniform(input_flows[1], (HEAD_COUNT, 1), jnp.float32, 30.0, 50.0)
    slow_rate = jnp.exp(jax.random.uniform(input_flows[2], (HEAD_COUNT, 1), jnp.float32, jnp.log(0.05), jnp.log(0.3))) / TOKEN_COUNT
    channel_factor = jnp.exp(jax.random.uniform(input_flows[3], (HEAD_COUNT, HEAD_WIDTH), jnp.float32, jnp.log(0.5), jnp.log(2.0)))
    baseline_rate = (jnp.where(fast_heads[:, None], fast_rate, slow_rate) * channel_factor).reshape(1, HEAD_COUNT * HEAD_WIDTH)
    block_count = TOKEN_COUNT // SPAN
    block_multiplier = jnp.exp(jax.random.uniform(input_flows[4], (block_count, HEAD_COUNT * HEAD_WIDTH), jnp.float32, jnp.log(0.5), jnp.log(2.0)))
    block_multiplier = jnp.repeat(block_multiplier, SPAN, axis=0)
    jaggedness = jax.random.uniform(input_flows[5], (TOKEN_COUNT, HEAD_COUNT * HEAD_WIDTH), jnp.float32, rough_low, rough_high)
    spike_position = jax.random.randint(input_flows[6], (2, HEAD_COUNT), 0, TOKEN_COUNT)
    spike_penalty = jax.random.uniform(input_flows[7], (2, HEAD_COUNT), jnp.float32, 0.223, 0.693)
    positions = jnp.arange(TOKEN_COUNT)[:, None]
    spike_events = jnp.where(positions == spike_position[0][None, :], spike_penalty[0][None, :], 0.0)
    spike_events = spike_events + jnp.where(positions == spike_position[1][None, :], spike_penalty[1][None, :], 0.0)
    spike_events = jnp.repeat(spike_events, HEAD_WIDTH, axis=1)
    final_output = -(baseline_rate * block_multiplier * jaggedness) - spike_events
    return final_output.astype(jnp.bfloat16)


def levels(stream_key, dims, pieces, smallest, high):
    level, own = 1.0, jax.random.fold_in(stream_key, 6)
    for axis_at, parts in pieces:
        draws = jnp.exp(jax.random.uniform(jax.random.fold_in(own, axis_at), (parts,), jnp.float32, smallest / len(pieces), high / len(pieces)))
        level = level * jnp.repeat(draws, dims[axis_at] // parts).reshape([-1 if axis == axis_at else 1 for axis in range(len(dims))])
    return level


def noise(own_key, shape, scale, limit, cuts=(), held_as=jnp.bfloat16):
    drawn = jax.random.normal(own_key, shape, jnp.float32) * scale
    if len(cuts) > 0:
        drawn = levels(own_key, shape, cuts, -0.22, 0.18) * drawn
    return jnp.clip(drawn, min=-limit, max=limit).astype(held_as)


def setup_inputs(seed: int = 0, part: int = 0) -> dict:
    splits = jax.random.split(jax.random.key(seed), 9)
    own_keys = jax.random.split(jax.random.fold_in(splits[8], part), 9)
    query_raw = noise(own_keys[0], (TOKEN_COUNT, HD), 1.0, 6.0, ((0, 16),))
    key_raw = draw_key_raw(jax.random.fold_in(jax.random.fold_in(splits[8], part), 71), part)
    value_raw = noise(own_keys[2], (TOKEN_COUNT, HD), 1.0, 6.0, ((0, 16),))
    log_decay = draw_log_decay(jax.random.fold_in(jax.random.fold_in(splits[8], part), 71), part)
    beta = draw_beta(jax.random.fold_in(jax.random.fold_in(splits[8], part), 71), part)
    conv_weight = noise(splits[5], (3, CONV, HD), CONV ** -0.5, 3.0, (), jnp.float32)
    out_gate = noise(own_keys[6], (TOKEN_COUNT, HD), 1.5, 6.0, ((0, 16),))
    norm_gain = jnp.clip(1.0 + 0.18 * jax.random.normal(splits[7], (HEAD_WIDTH,), jnp.float32), 0.1, 1.9)
    return dict(query_raw=query_raw, key_raw=key_raw, value_raw=value_raw, log_decay=log_decay, beta=beta, conv_weight=conv_weight, out_gate=out_gate, norm_gain=norm_gain)


def matmul(left, right):
    return jnp.einsum('...ij,...jk->...ik', left, right, precision=lax.Precision.HIGHEST)

def short_conv(values_in, rim_rows, taps):
    count = values_in.shape[0]
    width = taps.shape[0]
    padded = jnp.concatenate([rim_rows, values_in], 0).astype(jnp.float32)
    total = taps[0] * padded[0:count]
    for offset in range(1, width):
        total = total + taps[offset] * padded[offset:offset + count]
    return jax.nn.silu(total).astype(jnp.bfloat16)

def block_terms(query, keys, values, log_gate, rates):
    keys = keys * lax.rsqrt(lax.optimization_barrier(jnp.sum(keys * keys, -1, keepdims=True)) + 1e-06)
    cumul = jnp.cumsum(log_gate, axis=-2)
    last_cum = cumul[..., -1:, :]
    query_up = query * jnp.exp(cumul)
    key_up = keys * jnp.exp(cumul)
    key_down = keys * jnp.exp(-cumul)
    key_end = keys * jnp.exp(last_cum - cumul)
    length = query.shape[-2]
    positions = jnp.arange(length)
    strict = positions[:, None] > positions[None, :]
    weak = positions[:, None] >= positions[None, :]
    inner = jnp.einsum('...cd,...jd->...cj', key_up, key_down, precision=lax.Precision.HIGHEST)
    unit_lower = jnp.eye(length, dtype=jnp.float32) + jnp.where(strict, inner * rates[..., :, None], 0.0)
    right_side = jnp.concatenate([rates[..., None] * values, rates[..., None] * key_up], -1)
    solved = lax.linalg.triangular_solve(unit_lower, right_side, left_side=True, lower=True, unit_diagonal=True)
    width = values.shape[-1]
    update_rows = solved[..., :width]
    correct_rows = solved[..., width:]
    scores = jnp.where(weak, jnp.einsum('...cd,...jd->...cj', query_up, key_down, precision=lax.Precision.HIGHEST), 0.0)
    return (query_up, key_end, update_rows, correct_rows, scores, last_cum)

def finish(attention, gate_logits, gain):
    rows_count = attention.shape[0]
    heads_view = attention.astype(jnp.float32).reshape(rows_count, -1, HEAD_WIDTH)
    scale = lax.rsqrt(lax.optimization_barrier(jnp.mean(heads_view * heads_view, -1, keepdims=True)) + 1e-05)
    gate_view = jax.nn.sigmoid(gate_logits.astype(jnp.float32).reshape(rows_count, -1, HEAD_WIDTH))
    final_output = heads_view * scale * gain * gate_view
    return final_output.reshape(rows_count, -1).astype(jnp.bfloat16)

def reference(query_raw, key_raw, value_raw, log_decay, beta, conv_weight, out_gate, norm_gain):
    zero_rim = jnp.zeros((CONV - 1, HEAD_COUNT * HEAD_WIDTH), jnp.bfloat16)
    query_in = short_conv(query_raw, zero_rim, conv_weight[0])
    key_in = short_conv(key_raw, zero_rim, conv_weight[1])
    value_in = short_conv(value_raw, zero_rim, conv_weight[2])
    blocks_count = TOKEN_COUNT // STRETCH

    def blocks(array):
        return array.reshape(blocks_count, STRETCH, array.shape[1])

    def heads_first(array):
        return array.astype(jnp.float32).reshape(STRETCH, HEAD_COUNT, HEAD_WIDTH).transpose(1, 0, 2)

    def advance(state, inputs):
        query_c, key_c, value_c, gate_c, rate_c = inputs
        rates = rate_c.astype(jnp.float32).transpose(1, 0)
        query_up, key_end, update_rows, correct_rows, scores, last_cum = block_terms(heads_first(query_c), heads_first(key_c), heads_first(value_c), heads_first(gate_c), rates)
        written = update_rows - matmul(correct_rows, state)
        output = matmul(query_up, state) + matmul(scores, written)
        new_state = jnp.exp(last_cum)[:, 0, :, None] * state + jnp.einsum('hcd,hce->hde', key_end, written, precision=lax.Precision.HIGHEST)
        return (new_state, output.transpose(1, 0, 2).reshape(STRETCH, HEAD_COUNT * HEAD_WIDTH).astype(jnp.bfloat16))
    start_state = jnp.zeros((HEAD_COUNT, HEAD_WIDTH, HEAD_WIDTH), jnp.float32)
    _, attention = lax.scan(advance, start_state, (blocks(query_in), blocks(key_in), blocks(value_in), blocks(log_decay), blocks(beta)))
    attention = attention.reshape(TOKEN_COUNT, HEAD_COUNT * HEAD_WIDTH)
    return finish(attention, out_gate, norm_gain)
```

```python
import functools

import jax
import jax.numpy as jnp
from jax import lax
from jax.experimental import pallas as pl
from jax.experimental.pallas import tpu as pltpu
from jax.sharding import PartitionSpec as P

D = 128
SUB = 16
EDGE = 16
F32 = jnp.float32
BF16 = jnp.bfloat16
VMEM_LIMIT = 48 * 1024 * 1024


def dot(a, b):
    return jnp.dot(a, b, preferred_element_type=F32)


def dot_t(a, b):
    return lax.dot_general(a, b, (((1,), (1,)), ((), ())), preferred_element_type=F32)


def t_dot(a, b):
    return lax.dot_general(a, b, (((0,), (0,)), ((), ())), preferred_element_type=F32)


def split(x):
    hi = x.astype(BF16)
    return hi, (x - hi.astype(F32)).astype(BF16)


def dot3(a, b):
    a_hi, a_lo = a
    b_hi, b_lo = b
    rows = a_hi.shape[0]
    both = dot(jnp.concatenate([a_hi, a_lo], 0), b_hi)
    return both[:rows] + both[rows:] + dot(a_hi, b_lo)


def silu(u):
    return u / (1.0 + jnp.exp(-u))


def conv(x, taps):
    width = taps.shape[0]
    total = x * taps[width - 1 : width]
    for back in range(1, width):
        total = total + pltpu.roll(x, back, 0) * taps[width - 1 - back : width - back]
    return silu(total).astype(BF16).astype(F32)


def key_terms(keys, rates, up, down, mid, end):
    norm = lax.rsqrt(jnp.sum(keys * keys, -1, keepdims=True) + 1e-6)
    unit = keys * norm
    write = unit * rates * up
    write_hi, write_lo = split(write)
    low = unit * down
    low_hi, low_lo = split(low)
    return write_hi, write_lo, low_hi, low_lo, (write * mid).astype(BF16), (low * end).astype(BF16)


def iota(shape, dim):
    return lax.broadcasted_iota(jnp.int32, shape, dim)


def prepare_kernel(
    q_ref, k_ref, v_ref, g_ref, beta_ref, taps_ref,
    whi_ref, wlo_ref, lhi_ref, llo_ref, kin_ref, kend_ref, vb_ref, qup_ref, up_ref, down_ref, marks_ref,
):
    rows, cols = q_ref.shape
    heads = cols // D
    middle = rows // 2 - 1
    at, other = iota((rows, rows), 0), iota((rows, rows), 1)
    plus = jnp.where((other <= at) & (other > middle), 1.0, 0.0)
    minus = jnp.where((other > at) & (other <= middle), 1.0, 0.0)
    sums = dot((plus - minus).astype(BF16), g_ref[...])
    up = jnp.exp(sums)
    down = jnp.exp(-sums)
    up_ref[...] = up
    down_ref[...] = down
    mid = jnp.exp(g_ref[0:16, :].astype(F32)[0:1] - sums[0:1])
    end = up[rows - 1 : rows]
    marks_ref[...] = jnp.concatenate([mid, end] * 4, 0)
    qup_ref[...] = (conv(q_ref[...].astype(F32), taps_ref[0]) * up).astype(BF16)
    values = conv(v_ref[...].astype(F32), taps_ref[2])
    keys = conv(k_ref[...].astype(F32), taps_ref[1])
    base = pl.program_id(0) * heads
    rates = beta_ref[...].astype(F32)
    lane = iota(rates.shape, 1)
    for h in range(heads):
        c = slice(h * D, (h + 1) * D)
        rate = jnp.sum(jnp.where(lane == base + h, rates, 0.0), -1, keepdims=True)
        out = key_terms(keys[:, c], rate, up[:, c], down[:, c], mid[:, c], end[:, c])
        for ref, value in zip((whi_ref, wlo_ref, lhi_ref, llo_ref, kin_ref, kend_ref), out):
            ref[:, c] = value
        vb_ref[:, c] = (values[:, c] * rate).astype(BF16)


def edge_rows(rim, which, raw_ref, taps):
    width = taps.shape[0]
    first = which * (width - 1)
    before = pltpu.roll(rim, (8 - (width - 1) - first) % rim.shape[0], 0)[0:8]
    return conv(jnp.concatenate([before, raw_ref[...].astype(F32)], 0), taps)[8:]


def solve_heads(lows, rows):
    lane_sub = iota((SUB, rows), 1)
    blocks = rows // SUB
    at, other = iota((rows, rows), 0), iota((rows, rows), 1)
    same = (at // SUB) == (other // SUB)
    packed = []
    for low in lows:
        own = jnp.where(same, low, 0.0)
        total = own[0:SUB]
        for b in range(1, blocks):
            total = total + own[b * SUB : (b + 1) * SUB]
        packed.append(total)
    unit = jnp.where(lane_sub % SUB == iota((SUB, rows), 0), 1.0, 0.0)
    solved = [unit for _ in lows]
    group_start = lane_sub - lane_sub % SUB
    for j in range(SUB - 1):
        for n, total in enumerate(packed):
            spread = jnp.take_along_axis(total, group_start + j, axis=1, mode="promise_in_bounds")
            solved[n] = solved[n] - spread * solved[n][j : j + 1]
    full = [jnp.where(same, jnp.concatenate([x] * blocks, 0), 0.0) for x in solved]
    size = SUB
    while size < rows:
        mask = (at // (2 * size) == other // (2 * size)) & (at // size != other // size)
        lower = [slice(p * size, (p + 1) * size) for p in range(1, rows // size, 2)]
        take = lambda x: jnp.concatenate([x[s] for s in lower], 0)
        small_mask = take(mask)
        parts = [split(x) for x in full]
        links = [split(jnp.where(small_mask, take(low), 0.0)) for low in lows]
        inner = [dot3(link, part) for link, part in zip(links, parts)]
        zeros = jnp.zeros((size, rows), F32)
        spread = []
        for x in inner:
            pieces = []
            for p in range(rows // (2 * size)):
                pieces += [zeros, x[p * size : (p + 1) * size]]
            spread.append(split(jnp.concatenate(pieces, 0)))
        fixes = [dot3((take(part[0]), take(part[1])), s) for part, s in zip(parts, spread)]
        result = []
        for x, fix in zip(full, fixes):
            pieces = []
            for p in range(rows // (2 * size)):
                pieces += [
                    x[2 * p * size : (2 * p + 1) * size],
                    x[(2 * p + 1) * size : (2 * p + 2) * size] - fix[p * size : (p + 1) * size],
                ]
            result.append(jnp.concatenate(pieces, 0))
        full = result
        size *= 2
    return full


def block_kernel(
    group_ref, rim_ref, k_ref, v_ref, beta_ref, taps_ref, up_ref, down_ref, marks_ref,
    whi_ref, wlo_ref, lhi_ref, llo_ref, kin_ref, kend_ref, vb_ref,
    move_ref, rows_ref, low_ref,
):
    rows, cols = whi_ref.shape
    heads = cols // D
    rim = rim_ref[...].astype(F32)
    keys = edge_rows(rim, 1, k_ref, taps_ref[1])
    values = edge_rows(rim, 2, v_ref, taps_ref[2])
    rates = beta_ref[...].astype(F32)
    lane = iota(rates.shape, 1)
    base = group_ref[0] * heads
    at, other = iota((rows, rows), 0), iota((rows, rows), 1)
    lows, ends, sides = [], [], []
    for h in range(heads):
        c = slice(h * D, (h + 1) * D)
        rate = jnp.sum(jnp.where(lane == base + h, rates, 0.0), -1, keepdims=True)
        mid, end = marks_ref[0:1, c], marks_ref[1:2, c]
        edge = key_terms(keys[:, c], rate, up_ref[:, c], down_ref[:, c], mid, end)
        whole = [
            jnp.concatenate([e, ref[EDGE:, c]], 0)
            for e, ref in zip(edge, (whi_ref, wlo_ref, lhi_ref, llo_ref, kin_ref, kend_ref))
        ]
        vb = jnp.concatenate([(values[:, c] * rate).astype(BF16), vb_ref[EDGE:, c]], 0)
        whi, wlo, lhi, llo, kin, kend = whole
        low_ref[:, c] = lhi
        both = dot_t(jnp.concatenate([whi, wlo], 0), lhi)
        inner = both[:rows] + both[rows:] + dot_t(whi, llo)
        lows.append(jnp.where(at > other, inner, 0.0))
        ends.append(kend)
        sides.append(jnp.concatenate([kin, vb], 1))
    solved = solve_heads(lows, rows)
    made = [dot(t.astype(BF16), side).astype(BF16) for t, side in zip(solved, sides)]
    for h in range(heads):
        c = slice(h * D, (h + 1) * D)
        sums = t_dot(ends[h], made[h])
        fade = marks_ref[0:1, c] * marks_ref[1:2, c] - 1.0
        move = jnp.where(at == other, fade, 0.0) - sums[:, :D]
        rows_ref[h] = made[h]
        move_ref[h, :, :D] = move.astype(BF16)
        move_ref[h, :, D:] = sums[:, D:].astype(BF16)


def local_kernel(
    group_ref, rim_ref, q_ref, taps_ref, up_ref, marks_ref, qup_ref, low_ref, rows_ref, gate_ref, gain_ref,
    reach_ref, own_ref, scale_ref,
):
    rows, cols = qup_ref.shape
    heads = cols // D
    rim = rim_ref[...].astype(F32)
    edge = (edge_rows(rim, 0, q_ref, taps_ref[0]) * up_ref[...]).astype(BF16)
    at, other = iota((rows, rows), 0), iota((rows, rows), 1)
    for h in range(heads):
        c = slice(h * D, (h + 1) * D)
        qup = jnp.concatenate([edge[:, c], qup_ref[EDGE:, c]], 0)
        scores = jnp.where(at >= other, dot_t(qup, low_ref[:, c]), 0.0).astype(BF16)
        seen = dot(scores, rows_ref[h])
        reach_ref[:, c] = (qup.astype(F32) * marks_ref[0:1, c] - seen[:, :D]).astype(BF16)
        own_ref[:, c] = seen[:, D:]
        gate = gate_ref[:, c].astype(F32)
        scale_ref[:, c] = gain_ref[...] / (1.0 + jnp.exp(-gate))


def compose_kernel(me_ref, *refs):
    pieces, (before_ref, whole_ref) = refs[:-2], refs[-2:]
    count = len(pieces)
    heads = whole_ref.shape[0]
    for m in range(count):

        @pl.when(me_ref[0] == m)
        def _():
            order = [pieces[m ^ b] for b in range(count)]
            run = [order[0][h].astype(F32) for h in range(heads)]
            for b in range(1, count):
                for h in range(heads):
                    now = run[h].astype(BF16)
                    before_ref[b - 1, h] = now
                    step = order[b][h]
                    run[h] = run[h] + step.astype(F32) + dot(step[:, :D], now)
            for h in range(heads):
                whole_ref[h] = run[h].astype(BF16)


def absorb_kernel(count, wide, last, *refs):
    parts, rest = refs[:count], refs[count:]
    have_ref = rest[0] if wide else None
    own_ref = rest[1] if wide else rest[0]
    outs = rest[2:] if wide else rest[1:]
    heads = own_ref.shape[0]
    for h in range(heads):
        now = parts[0][h]
        for ref in parts[1:]:
            now = now + ref[h]
        if wide:
            have = have_ref[h]
            now = (have.astype(F32) + now.astype(F32) + dot(have[:, :D], now)).astype(BF16)
            outs[1][h] = now
        own = own_ref[h]
        send = now[:, D:] if last else now
        after = send.astype(F32) + (own[:, D:] if last else own).astype(F32) + dot(own[:, :D], send)
        outs[0][h] = after.astype(BF16)


def starts_kernel(count, me_ref, *refs):
    came_refs, have_ref, before_ref, outs = refs[:count], refs[count], refs[count + 1], refs[count + 2 :]
    heads = have_ref.shape[0]
    first = []
    for h in range(heads):
        came = came_refs[0][h]
        for ref in came_refs[1:]:
            came = came + ref[h]
        have = have_ref[h]
        first.append(have[:, D:].astype(F32) + came.astype(F32) + dot(have[:, :D], came))
    later = []
    for b in range(1, len(outs)):
        for h in range(heads):
            known = before_ref[b - 1, h]
            later.append(
                (first[h] + known[:, D:].astype(F32) + dot(known[:, :D], first[h].astype(BF16))).astype(BF16)
            )
    for m in range(len(outs)):

        @pl.when(me_ref[0] == m)
        def _():
            for b in range(len(outs)):
                for h in range(heads):
                    outs[m ^ b][h] = first[h].astype(BF16) if b == 0 else later[(b - 1) * heads + h]


def finish_kernel(count, me_ref, *refs):
    out_ref = refs[-1]
    reach, own, scale, starts = (refs[k * count : (k + 1) * count] for k in range(4))
    heads = starts[0].shape[0]
    for m in range(count):

        @pl.when(me_ref[0] == m)
        def _():
            for g in range(count):
                j = m ^ g
                for h in range(heads):
                    c = slice(h * D, (h + 1) * D)
                    found = own[j][:, c] + dot(reach[j][:, c], starts[j][h])
                    found = found.astype(BF16).astype(F32)
                    mean = jnp.mean(found * found, -1, keepdims=True)
                    at = slice((g * heads + h) * D, (g * heads + h + 1) * D)
                    out_ref[:, at] = (found * lax.rsqrt(mean + 1e-5) * scale[j][:, c]).astype(BF16)


def params():
    return pltpu.CompilerParams(vmem_limit_bytes=VMEM_LIMIT)


def shards(query_raw, key_raw, value_raw, log_decay, beta, conv_weight, out_gate, norm_gain):
    rows, width = query_raw.shape
    groups = lax.axis_size("head")
    spans = lax.axis_size("ctx")
    cols = width // groups
    heads = cols // D
    rim_width = conv_weight.shape[1] - 1
    me = lax.axis_index("head")
    me_arg = me.reshape(1).astype(jnp.int32)

    tails = jnp.concatenate(
        [query_raw[-rim_width:], key_raw[-rim_width:], value_raw[-rim_width:]]
        + [jnp.zeros((16 - 3 * rim_width, width), BF16)],
        0,
    )
    total = groups * spans
    rim = lax.ppermute(tails, ("ctx", "head"), [(i, i + 1) for i in range(total - 1)])

    column = lambda i: (0, i)
    whole_block = pl.BlockSpec((rows, cols), column)
    taps_block = pl.BlockSpec(conv_weight.shape[:2] + (cols,), lambda i: (0, 0, i))
    wide16 = jax.ShapeDtypeStruct((rows, width), BF16)
    wide32 = jax.ShapeDtypeStruct((rows, width), F32)
    prepared = pl.pallas_call(
        prepare_kernel,
        grid=(groups,),
        in_specs=[whole_block] * 4 + [pl.BlockSpec(beta.shape, lambda i: (0, 0)), taps_block],
        out_specs=[whole_block] * 10 + [pl.BlockSpec((8, cols), column)],
        out_shape=[wide16] * 8 + [wide32] * 2 + [jax.ShapeDtypeStruct((8, width), F32)],
        compiler_params=params(),
        cost_estimate=pl.CostEstimate(flops=20_000_000, bytes_accessed=9_000_000, transcendentals=2_000_000),
        name="prepare",
    )(query_raw, key_raw, value_raw, log_decay, beta, conv_weight)
    whi, wlo, lhi, llo, kin, kend, vb, qup, up, down, marks = prepared

    dyn = lambda i, g: (0, g[0])
    edge_block = pl.BlockSpec((EDGE, cols), dyn)
    rows_block = pl.BlockSpec((rows, cols), dyn)
    marks_block = pl.BlockSpec((8, cols), dyn)
    taps_dyn = pl.BlockSpec(conv_weight.shape[:2] + (cols,), lambda i, g: (0, 0, g[0]))
    head_block = pl.BlockSpec((heads, rows, 2 * D), lambda i, g: (0, 0, 0))
    still = pl.BlockSpec((rows, cols), lambda i, g: (0, 0))
    moves, made, lows = [None] * groups, [None] * groups, [None] * groups
    order = list(range(groups - 1, -1, -1))
    for j in order:
        moves[j], made[j], lows[j] = pl.pallas_call(
            block_kernel,
            grid_spec=pltpu.PrefetchScalarGridSpec(
                num_scalar_prefetch=1,
                grid=(1,),
                in_specs=[
                    edge_block, edge_block, edge_block,
                    pl.BlockSpec((EDGE, beta.shape[1]), lambda i, g: (0, 0)),
                    taps_dyn, edge_block, edge_block, marks_block,
                ]
                + [rows_block] * 7,
                out_specs=[head_block, head_block, still],
            ),
            out_shape=[
                jax.ShapeDtypeStruct((heads, D, 2 * D), BF16),
                jax.ShapeDtypeStruct((heads, rows, 2 * D), BF16),
                jax.ShapeDtypeStruct((rows, cols), BF16),
            ],
            compiler_params=params(),
            name="block",
        )(me_arg ^ j, rim, key_raw, value_raw, beta, conv_weight, up, down, marks, whi, wlo, lhi, llo, kin, kend, vb)

    def swap(array, j):
        return lax.ppermute(array, "head", [(i, i ^ j) for i in range(groups)])

    came = [moves[0]] + [None] * (groups - 1)
    for j in order[:-1]:
        came[j] = swap(moves[j], j)

    local = []
    for j in range(groups):
        local.append(
            pl.pallas_call(
                local_kernel,
                grid_spec=pltpu.PrefetchScalarGridSpec(
                    num_scalar_prefetch=1,
                    grid=(1,),
                    in_specs=[
                        edge_block, edge_block, taps_dyn, edge_block, marks_block, rows_block,
                        still, head_block, rows_block, pl.BlockSpec((1, D), lambda i, g: (0, 0)),
                    ],
                    out_specs=[still] * 3,
                ),
                out_shape=[
                    jax.ShapeDtypeStruct((rows, cols), BF16),
                    jax.ShapeDtypeStruct((rows, cols), F32),
                    jax.ShapeDtypeStruct((rows, cols), F32),
                ],
                compiler_params=params(),
                name="local",
            )(me_arg ^ j, rim, query_raw, conv_weight, up, marks, qup, lows[j], made[j], out_gate, norm_gain.reshape(1, D))
        )

    smem = pl.BlockSpec(memory_space=pltpu.SMEM)
    vmem = pl.BlockSpec(memory_space=pltpu.VMEM)
    pair = jax.ShapeDtypeStruct((heads, D, 2 * D), BF16)
    before, whole = pl.pallas_call(
        compose_kernel,
        in_specs=[smem] + [vmem] * groups,
        out_specs=[vmem, vmem],
        out_shape=[jax.ShapeDtypeStruct((groups - 1, heads, D, 2 * D), BF16), pair],
        compiler_params=params(),
        name="compose",
    )(me_arg, *came)

    state = jax.ShapeDtypeStruct((heads, D, D), BF16)
    have, send, half = None, whole if spans > 2 else whole[:, :, D:], 1
    parts = [jnp.zeros((heads, D, D), BF16)]
    while half < spans:
        parts = []
        for step in range(1, half + 1):
            route = [
                (low + half - 1, low + half - 1 + step)
                for low in range(0, spans, 2 * half)
                if low + half - 1 + step < spans
            ]
            parts.append(lax.ppermute(send, "ctx", route))
        half *= 2
        if half < spans:
            wide, last = have is not None, 2 * half >= spans
            kept = [have] if wide else []
            got = pl.pallas_call(
                functools.partial(absorb_kernel, len(parts), wide, last),
                in_specs=[vmem] * (len(parts) + len(kept) + 1),
                out_specs=[vmem] * (1 + len(kept)),
                out_shape=[state if last else pair] + [pair] * len(kept),
                compiler_params=params(),
                name="absorb",
            )(*parts, *kept, whole)
            send, have = got[0], got[1] if wide else parts[0]
    if have is None:
        have = jnp.zeros((heads, D, 2 * D), BF16)

    starts = pl.pallas_call(
        functools.partial(starts_kernel, len(parts)),
        in_specs=[smem] + [vmem] * (len(parts) + 2),
        out_specs=[vmem] * groups,
        out_shape=[state] * groups,
        compiler_params=params(),
        name="starts",
    )(me_arg, *parts, have, before)
    starts = [starts[0]] + [swap(starts[j], j) for j in range(1, groups)]

    reach, own, scale = zip(*local)
    return pl.pallas_call(
        functools.partial(finish_kernel, groups),
        in_specs=[smem] + [vmem] * (4 * groups),
        out_specs=vmem,
        out_shape=wide16,
        compiler_params=params(),
        name="finish",
    )(me_arg, *reach, *own, *scale, *starts)


def solution(mesh):
    tokens = P(("dp", "ctx", "head"), None)
    placed = (tokens, tokens, tokens, tokens, tokens, P(), tokens, P())
    return jax.shard_map(shards, mesh=mesh, in_specs=placed, out_specs=tokens, check_vma=False)
```

```python
import functools

import jax
import jax.numpy as jnp
from jax import lax
from jax.experimental import pallas as pl
from jax.experimental.pallas import tpu as pltpu
from jax.sharding import PartitionSpec as P

D = 128
SUB = 16
EDGE = 16
F32 = jnp.float32
BF16 = jnp.bfloat16
VMEM_LIMIT = 32 * 1024 * 1024


def dot(a, b):
    return jnp.dot(a, b, preferred_element_type=F32)


def dot_t(a, b):
    return lax.dot_general(a, b, (((1,), (1,)), ((), ())), preferred_element_type=F32)


def t_dot(a, b):
    return lax.dot_general(a, b, (((0,), (0,)), ((), ())), preferred_element_type=F32)


def split(x):
    hi = x.astype(BF16)
    return hi, (x - hi.astype(F32)).astype(BF16)


def dot3(a, b):
    a_hi, a_lo = a
    b_hi, b_lo = b
    rows = a_hi.shape[0]
    both = dot(jnp.concatenate([a_hi, a_lo], 0), b_hi)
    return both[:rows] + both[rows:] + dot(a_hi, b_lo)


def silu(u):
    return u / (1.0 + jnp.exp(-u))


def conv(x, taps):
    width = taps.shape[0]
    total = x * taps[width - 1 : width]
    for back in range(1, width):
        total = total + pltpu.roll(x, back, 0) * taps[width - 1 - back : width - back]
    return silu(total).astype(BF16).astype(F32)


def key_terms(keys, rates, up, down, mid, end):
    norm = lax.rsqrt(jnp.sum(keys * keys, -1, keepdims=True) + 1e-6)
    unit = keys * norm
    write = unit * rates * up
    low = unit * down
    return (write.astype(BF16), low.astype(BF16), (write * mid).astype(BF16)) + split(low * end)


def iota(shape, dim):
    return lax.broadcasted_iota(jnp.int32, shape, dim)


def tails_kernel(width, *refs):
    ins, out_ref, held, sems = refs[:3], refs[3], refs[4], refs[5]
    rows = ins[0].shape[0]
    copies = [
        pltpu.make_async_copy(ref.at[pl.ds(rows - EDGE, EDGE)], held.at[n], sems.at[n]) for n, ref in enumerate(ins)
    ]
    for copy in copies:
        copy.start()
    parts = []
    for n, copy in enumerate(copies):
        copy.wait()
        parts.append(held[n].astype(F32)[EDGE - width :])
    parts.append(jnp.zeros((EDGE - 3 * width, out_ref.shape[1]), F32))
    out_ref[...] = jnp.concatenate(parts, 0).astype(BF16)


def prepare_kernel(
    groups, g_ref, k_ref, v_ref, beta_ref, taps_ref,
    write_ref, low_ref, kin_ref, khi_ref, klo_ref, vb_ref, up_ref, down_ref, marks_ref, edge_ref, rates_ref,
    held, sems,
):
    rows, width = g_ref.shape
    cols = width // groups
    heads = cols // D
    copies = {}
    for i in range(groups):
        for n, ref in enumerate((g_ref, k_ref, v_ref)):
            c = pl.ds(i * cols, cols)
            copies[n, i] = pltpu.make_async_copy(ref.at[:, c], held.at[n, :, c], sems.at[n, i])
            copies[n, i].start()
    middle = rows // 2 - 1
    at, other = iota((rows, rows), 0), iota((rows, rows), 1)
    plus = jnp.where((other <= at) & (other > middle), 1.0, 0.0)
    minus = jnp.where((other > at) & (other <= middle), 1.0, 0.0)
    summing = (plus - minus).astype(BF16)
    rates = beta_ref[...].astype(F32).T
    rates_ref[...] = rates[:EDGE]
    lane = iota(rates.shape, 1)
    for i in range(groups):
        whole = slice(i * cols, (i + 1) * cols)
        copies[0, i].wait()
        sums = dot(summing, held[0, :, whole])
        up = jnp.exp(sums)
        down = jnp.exp(-sums)
        up_ref[:, whole] = up
        down_ref[:, whole] = down[:EDGE]
        mid = jnp.exp(held[0, 0:EDGE, whole].astype(F32)[0:1] - sums[0:1])
        end = up[rows - 1 : rows]
        marks_ref[:, whole] = jnp.concatenate([mid, end] * 4, 0)
        copies[1, i].wait()
        edge_ref[0, :, whole] = held[1, 0:EDGE, whole]
        keys = conv(held[1, :, whole].astype(F32), taps_ref[1, :, whole])
        for h in range(heads):
            c = slice(h * D, (h + 1) * D)
            to = slice((i * heads + h) * D, (i * heads + h + 1) * D)
            rate = jnp.sum(jnp.where(lane == i * heads + h, rates, 0.0), -1, keepdims=True)
            out = key_terms(keys[:, c], rate, up[:, c], down[:, c], mid[:, c], end[:, c])
            for ref, value in zip((write_ref, low_ref, kin_ref, khi_ref, klo_ref), out):
                ref[:, to] = value
        copies[2, i].wait()
        edge_ref[1, :, whole] = held[2, 0:EDGE, whole]
        values = conv(held[2, :, whole].astype(F32), taps_ref[2, :, whole])
        for h in range(heads):
            to = slice((i * heads + h) * D, (i * heads + h + 1) * D)
            rate = jnp.sum(jnp.where(lane == i * heads + h, rates, 0.0), -1, keepdims=True)
            vb_ref[:, to] = (values[:, h * D : (h + 1) * D] * rate).astype(BF16)


def edge_rows(rim, which, raw, taps):
    width = taps.shape[0]
    first = which * (width - 1)
    before = pltpu.roll(rim, (8 - (width - 1) - first) % rim.shape[0], 0)[0:8]
    return conv(jnp.concatenate([before, raw.astype(F32)], 0), taps)[8:]


def solve_heads(lows, rows):
    lane_sub = iota((SUB, rows), 1)
    blocks = rows // SUB
    at, other = iota((rows, rows), 0), iota((rows, rows), 1)
    same = (at // SUB) == (other // SUB)
    packed = []
    for low in lows:
        own = jnp.where(same, low, 0.0)
        total = own[0:SUB]
        for b in range(1, blocks):
            total = total + own[b * SUB : (b + 1) * SUB]
        packed.append(total)
    unit = jnp.where(lane_sub % SUB == iota((SUB, rows), 0), 1.0, 0.0)
    solved = [unit for _ in lows]
    group_start = lane_sub - lane_sub % SUB
    for j in range(SUB - 1):
        for n, total in enumerate(packed):
            spread = jnp.take_along_axis(total, group_start + j, axis=1, mode="promise_in_bounds")
            solved[n] = solved[n] - spread * solved[n][j : j + 1]
    full = [jnp.where(same, jnp.concatenate([x] * blocks, 0), 0.0) for x in solved]
    size = SUB
    while size < rows:
        mask = (at // (2 * size) == other // (2 * size)) & (at // size != other // size)
        lower = [slice(p * size, (p + 1) * size) for p in range(1, rows // size, 2)]
        take = lambda x: jnp.concatenate([x[s] for s in lower], 0)
        small_mask = take(mask)
        parts = [split(x) for x in full]
        links = [split(jnp.where(small_mask, take(low), 0.0)) for low in lows]
        inner = [dot3(link, part) for link, part in zip(links, parts)]
        zeros = jnp.zeros((size, rows), F32)
        spread = []
        for x in inner:
            pieces = []
            for p in range(rows // (2 * size)):
                pieces += [zeros, x[p * size : (p + 1) * size]]
            spread.append(split(jnp.concatenate(pieces, 0)))
        fixes = [dot3((take(part[0]), take(part[1])), s) for part, s in zip(parts, spread)]
        result = []
        for x, fix in zip(full, fixes):
            pieces = []
            for p in range(rows // (2 * size)):
                pieces += [
                    x[2 * p * size : (2 * p + 1) * size],
                    x[(2 * p + 1) * size : (2 * p + 2) * size] - fix[p * size : (p + 1) * size],
                ]
            result.append(jnp.concatenate(pieces, 0))
        full = result
        size *= 2
    return full


def block_kernel(
    group_ref, later_ref, rim_ref, edge_ref, rates_ref, taps_ref, up_ref, down_ref, marks_ref,
    write_ref, low_ref, kin_ref, khi_ref, klo_ref, vb_ref,
    move_ref, made_ref, low_out_ref,
):
    rows = low_ref.shape[0]
    heads = move_ref.shape[0]
    cols = heads * D
    start = pl.multiple_of(group_ref[0] * cols, cols)
    mine = pl.ds(start, cols)
    rim = jnp.where(later_ref[0] > 0, rim_ref[:, mine].astype(F32), 0.0)
    keys = edge_rows(rim, 1, edge_ref[0, :, mine], taps_ref[1, :, mine])
    values = edge_rows(rim, 2, edge_ref[1, :, mine], taps_ref[2, :, mine])
    up, down, marks = up_ref[0:EDGE, mine], down_ref[:, mine], marks_ref[:, mine]
    rates = rates_ref[...]
    lane = iota(rates.shape, 1)
    base = group_ref[0] * heads
    at, other = iota((rows, rows), 0), iota((rows, rows), 1)
    lows, ends, sides = [], [], []
    for h in range(heads):
        c = slice(h * D, (h + 1) * D)
        here = pl.ds(pl.multiple_of(start + h * D, D), D)
        rate = jnp.sum(jnp.where(lane == base + h, rates, 0.0), -1, keepdims=True)
        edge = key_terms(keys[:, c], rate, up[:, c], down[:, c], marks[0:1, c], marks[1:2, c])
        write, low, kin, khi, klo = [
            jnp.concatenate([e, ref[EDGE:, here]], 0)
            for e, ref in zip(edge, (write_ref, low_ref, kin_ref, khi_ref, klo_ref))
        ]
        vb = jnp.concatenate([(values[:, c] * rate).astype(BF16), vb_ref[EDGE:, here]], 0)
        low_out_ref[:, c] = low
        lows.append(jnp.where(at > other, dot_t(write, low), 0.0))
        ends.append((khi, klo))
        sides.append(jnp.concatenate([kin, vb], 1))
    solved = solve_heads(lows, rows)
    made = []
    for t, side in zip(solved, sides):
        both = dot(jnp.concatenate(split(t), 0), side)
        made.append((both[:rows] + both[rows:]).astype(BF16))
    for h in range(heads):
        c = slice(h * D, (h + 1) * D)
        sums = t_dot(ends[h][0], made[h]) + t_dot(ends[h][1], made[h])
        fade = marks[0:1, c] * marks[1:2, c] - 1.0
        move = jnp.where(at == other, fade, 0.0) - sums[:, :D]
        made_ref[h] = made[h]
        move_ref[h, :, :D] = move.astype(BF16)
        move_ref[h, :, D:] = sums[:, D:].astype(BF16)


def local_kernel(count, later_ref, *refs):
    group_refs, refs = refs[:count], refs[count:]
    rim_ref, q_ref, gate_ref, taps_ref, gain_ref, up_ref, marks_ref, *refs = refs
    ins, outs, held, sems = refs[: 2 * count], refs[2 * count : 5 * count], refs[-2], refs[-1]
    rows, cols = outs[0].shape
    heads = cols // D
    starts = [pl.multiple_of(group_refs[i][0] * cols, cols) for i in range(count)]
    copies = {}
    for i in range(count):
        for n, ref in enumerate((q_ref, gate_ref)):
            copies[n, i] = pltpu.make_async_copy(ref.at[:, pl.ds(starts[i], cols)], held.at[n, i], sems.at[n, i])
            copies[n, i].start()
    at, other = iota((rows, rows), 0), iota((rows, rows), 1)
    for i in range(count):
        low_ref, made_ref = ins[2 * i : 2 * i + 2]
        reach_ref, own_ref, scale_ref = outs[3 * i : 3 * i + 3]
        mine = pl.ds(starts[i], cols)
        taps = taps_ref[0, :, mine]
        rim = jnp.where(later_ref[0] > 0, rim_ref[:, mine].astype(F32), 0.0)
        mid = marks_ref[0:1, mine]
        copies[0, i].wait()
        edge = edge_rows(rim, 0, held[0, i, 0:EDGE], taps)
        queries = jnp.concatenate([edge, conv(held[0, i].astype(F32), taps)[EDGE:]], 0) * up_ref[:, mine]
        copies[1, i].wait()
        gate = held[1, i].astype(F32)
        for h in range(heads):
            c = slice(h * D, (h + 1) * D)
            scores = jnp.where(at >= other, dot_t(queries[:, c].astype(BF16), low_ref[:, c]), 0.0)
            both = dot(jnp.concatenate(split(scores), 0), made_ref[h])
            seen = both[:rows] + both[rows:]
            reach_ref[:, c] = (queries[:, c] * mid[:, c] - seen[:, :D]).astype(BF16)
            own_ref[:, c] = seen[:, D:]
            scale_ref[:, c] = gain_ref[...] / (1.0 + jnp.exp(-gate[:, c]))


def follow(pair, state):
    add = pair[:, D:] if state.shape[1] == D else pair
    return (state.astype(F32) + add.astype(F32) + dot(pair[:, :D], state)).astype(BF16)


def chain_kernel(me_ref, *refs):
    pairs, before_ref, whole_ref = refs[:-2], refs[-2], refs[-1]
    count = len(pairs)
    heads = whole_ref.shape[0]
    for m in range(count):

        @pl.when(me_ref[0] == m)
        def _():
            now = [pairs[m][h] for h in range(heads)]
            for b in range(1, count):
                for h in range(heads):
                    before_ref[b - 1, h] = now[h]
                    now[h] = follow(pairs[m ^ b][h], now[h])
            for h in range(heads):
                whole_ref[h] = now[h]


def absorb_kernel(wide, last, upper_ref, mine_ref, theirs_ref, *refs):
    have_ref, (send_ref, ahead_ref) = (refs[0], refs[1:]) if wide else (None, refs)
    part = slice(D, 2 * D) if last else slice(0, 2 * D)
    heads = mine_ref.shape[0]
    for upper in (0, 1):

        @pl.when(upper_ref[0] == upper)
        def _():
            for h in range(heads):
                mine, theirs = mine_ref[h], theirs_ref[h]
                first, then = (theirs, mine) if upper else (mine, theirs)
                send_ref[h] = follow(then, first[:, part])
                if upper:
                    ahead_ref[h] = follow(have_ref[h], theirs) if wide else theirs
                else:
                    ahead_ref[h] = have_ref[h] if wide else jnp.zeros(theirs.shape, BF16)


def starts_kernel(me_ref, upper_ref, came_ref, ahead_ref, before_ref, *outs):
    heads = came_ref.shape[0]
    first = []
    for h in range(heads):
        came = jnp.where(upper_ref[0] > 0, came_ref[h].astype(F32), 0.0).astype(BF16)
        first.append(follow(ahead_ref[h], came))
    for m in range(len(outs)):

        @pl.when(me_ref[0] == m)
        def _():
            for b in range(len(outs)):
                for h in range(heads):
                    outs[m ^ b][h] = follow(before_ref[b - 1, h], first[h]) if b else first[h]


def finish_kernel(count, me_ref, *refs):
    out_ref = refs[-1]
    reach, own, scale, starts = (refs[k * count : (k + 1) * count] for k in range(4))
    heads = starts[0].shape[0]
    for m in range(count):

        @pl.when(me_ref[0] == m)
        def _():
            for g in range(count):
                j = m ^ g
                for h in range(heads):
                    c = slice(h * D, (h + 1) * D)
                    found = own[j][:, c] + dot(reach[j][:, c], starts[j][h])
                    found = found.astype(BF16).astype(F32)
                    mean = jnp.mean(found * found, -1, keepdims=True)
                    at = slice((g * heads + h) * D, (g * heads + h + 1) * D)
                    out_ref[:, at] = (found * lax.rsqrt(mean + 1e-5) * scale[j][:, c]).astype(BF16)


def params():
    return pltpu.CompilerParams(vmem_limit_bytes=VMEM_LIMIT)


def shards(query_raw, key_raw, value_raw, log_decay, beta, conv_weight, out_gate, norm_gain):
    rows, width = query_raw.shape
    groups = lax.axis_size("head")
    spans = lax.axis_size("ctx")
    cols = width // groups
    heads = cols // D
    rim_width = conv_weight.shape[1] - 1
    me = lax.axis_index("head").astype(jnp.int32).reshape(1)
    span = lax.axis_index("ctx").astype(jnp.int32).reshape(1)
    group_ids = [me ^ j for j in range(groups)]
    later = (me + span > 0).astype(jnp.int32)
    uppers = [(span >> bit) & 1 for bit in range((spans - 1).bit_length())]
    (group_ids, later, uppers), query_raw, key_raw, value_raw, log_decay = lax.optimization_barrier(
        ((group_ids, later, uppers), query_raw, key_raw, value_raw, log_decay)
    )
    me_arg = group_ids[0]
    query_raw, key_raw, value_raw, log_decay, out_gate = (
        pltpu.with_memory_space_constraint(x, pltpu.HBM) for x in (query_raw, key_raw, value_raw, log_decay, out_gate)
    )
    beta = beta.T

    smem = pl.BlockSpec(memory_space=pltpu.SMEM)
    vmem = pl.BlockSpec(memory_space=pltpu.VMEM)
    far = pl.BlockSpec(memory_space=pl.ANY)

    tails = pl.pallas_call(
        functools.partial(tails_kernel, rim_width),
        in_specs=[far] * 3,
        out_specs=vmem,
        out_shape=jax.ShapeDtypeStruct((EDGE, width), BF16),
        scratch_shapes=[pltpu.VMEM((3, EDGE, width), BF16), pltpu.SemaphoreType.DMA((3,))],
        compiler_params=params(),
        name="tails",
    )(query_raw, key_raw, value_raw)
    total = groups * spans
    rim = lax.ppermute(tails, ("ctx", "head"), [(i, (i + 1) % total) for i in range(total)])

    wide16 = jax.ShapeDtypeStruct((rows, width), BF16)
    prepared = pl.pallas_call(
        functools.partial(prepare_kernel, groups),
        in_specs=[far] * 3 + [vmem] * 2,
        out_specs=[vmem] * 11,
        out_shape=[wide16] * 6
        + [
            jax.ShapeDtypeStruct((rows, width), F32),
            jax.ShapeDtypeStruct((EDGE, width), F32),
            jax.ShapeDtypeStruct((8, width), F32),
            jax.ShapeDtypeStruct((2, EDGE, width), BF16),
            jax.ShapeDtypeStruct((EDGE, beta.shape[0]), F32),
        ],
        scratch_shapes=[pltpu.VMEM((3, rows, width), BF16), pltpu.SemaphoreType.DMA((3, groups))],
        compiler_params=params(),
        cost_estimate=pl.CostEstimate(flops=20_000_000, bytes_accessed=9_000_000, transcendentals=2_000_000),
        name="prepare",
    )(log_decay, key_raw, value_raw, beta, conv_weight)
    write, low, kin, khi, klo, vb, up, down, marks, edges, rates = prepared

    moves, made, lows = [None] * groups, [None] * groups, [None] * groups
    order = list(range(groups - 1, -1, -1))
    for j in order:
        moves[j], made[j], lows[j] = pl.pallas_call(
            block_kernel,
            in_specs=[smem] * 2 + [vmem] * 13,
            out_specs=[vmem] * 3,
            out_shape=[
                jax.ShapeDtypeStruct((heads, D, 2 * D), BF16),
                jax.ShapeDtypeStruct((heads, rows, 2 * D), BF16),
                jax.ShapeDtypeStruct((rows, cols), BF16),
            ],
            compiler_params=params(),
            name="block",
        )(group_ids[j], later, rim, edges, rates, conv_weight, up, down, marks, write, low, kin, khi, klo, vb)

    def call(kernel, name, in_specs, outs, scratch=()):
        return pl.pallas_call(
            kernel,
            in_specs=in_specs,
            out_specs=[vmem] * len(outs),
            out_shape=[jax.ShapeDtypeStruct(*out) for out in outs],
            scratch_shapes=scratch,
            compiler_params=params(),
            name=name,
        )

    def swap(array, j, axis="head"):
        return lax.ppermute(array, axis, [(i, i ^ j) for i in range(lax.axis_size(axis))])

    block16, block32 = ((rows, cols), BF16), ((rows, cols), F32)
    state, pair = ((heads, D, D), BF16), ((heads, D, 2 * D), BF16)

    def local(js):
        if not js:
            return {}
        got = call(
            functools.partial(local_kernel, len(js)),
            "local",
            [smem] * (1 + len(js)) + [vmem, far, far] + [vmem] * (4 + 2 * len(js)),
            [block16, block32, block32] * len(js),
            [pltpu.VMEM((2, len(js), rows, cols), BF16), pltpu.SemaphoreType.DMA((2, len(js)))],
        )(
            later, *[group_ids[j] for j in js], rim, query_raw, out_gate, conv_weight, norm_gain.reshape(1, D),
            up, marks, *[x for j in js for x in (lows[j], made[j])],
        )
        return {j: got[3 * i : 3 * i + 3] for i, j in enumerate(js)}

    came_pairs = [swap(moves[j], j) if j else moves[j] for j in range(groups)]
    left = list(range(groups))
    came_pairs, found = lax.optimization_barrier((came_pairs, local(left[: groups // 2])))
    left = left[groups // 2 :]

    before, whole = call(
        chain_kernel, "chain", [smem] + [vmem] * groups, [((groups - 1, heads, D, 2 * D), BF16), pair]
    )(me_arg, *came_pairs)

    ahead, bit, send = None, 1, whole if spans > 2 else whole[:, :, D:]
    came, upper = None, later
    while bit < spans:
        last = 2 * bit >= spans
        theirs = swap(send, bit, "ctx")
        if left:
            theirs, mine = lax.optimization_barrier((theirs, local(left)))
            found.update(mine)
            left = []
        upper = uppers[bit.bit_length() - 1]
        if last:
            came = theirs
        else:
            wide, next_last = ahead is not None, 4 * bit >= spans
            send, ahead = call(
                functools.partial(absorb_kernel, wide, next_last),
                "absorb",
                [smem] + [vmem] * (3 if wide else 2),
                [state if next_last else pair, pair],
            )(upper, whole, theirs, *([ahead] if wide else []))
            whole = send
        bit *= 2
    found.update(local(left))
    came = jnp.zeros(*state) if came is None else came
    ahead = jnp.zeros(*pair) if ahead is None else ahead

    starts = call(starts_kernel, "starts", [smem] * 2 + [vmem] * 3, [state] * groups)(
        me_arg, upper, came, ahead, before
    )
    starts = [starts[0]] + [swap(starts[j], j) for j in range(1, groups)]

    reach, own, scale = zip(*[found[j] for j in range(groups)])
    (out,) = call(
        functools.partial(finish_kernel, groups),
        "finish",
        [smem] + [vmem] * (4 * groups),
        [((rows, width), BF16)],
    )(me_arg, *reach, *own, *scale, *starts)
    return out


def solution(mesh):
    tokens = P(("dp", "ctx", "head"), None)
    placed = (tokens, tokens, tokens, tokens, tokens, P(), tokens, P())
    return jax.shard_map(shards, mesh=mesh, in_specs=placed, out_specs=tokens, check_vma=False)
```

```python
import functools
import itertools

import jax
import jax.numpy as jnp
from jax import lax
from jax.experimental import pallas as pl
from jax.experimental.pallas import tpu as pltpu
from jax.sharding import PartitionSpec as P

D = 128
SUB = 16
EDGE = 16
F32 = jnp.float32
BF16 = jnp.bfloat16
FIRST = 1
VMEM_LIMIT = 32 * 1024 * 1024


def dot(a, b):
    return jnp.dot(a, b, preferred_element_type=F32)


def dot_t(a, b):
    return lax.dot_general(a, b, (((1,), (1,)), ((), ())), preferred_element_type=F32)


def t_dot(a, b):
    return lax.dot_general(a, b, (((0,), (0,)), ((), ())), preferred_element_type=F32)


def split(x):
    hi = x.astype(BF16)
    return hi, (x - hi.astype(F32)).astype(BF16)


def dot3(a, b):
    a_hi, a_lo = a
    b_hi, b_lo = b
    rows = a_hi.shape[0]
    both = dot(jnp.concatenate([a_hi, a_lo], 0), b_hi)
    return both[:rows] + both[rows:] + dot(a_hi, b_lo)


def silu(u):
    half = 0.5 * u
    return half + half * jnp.tanh(half)


def conv(x, taps):
    width = taps.shape[0]
    total = x * taps[width - 1 : width]
    for back in range(1, width):
        total = total + pltpu.roll(x, back, 0) * taps[width - 1 - back : width - back]
    return silu(total).astype(BF16).astype(F32)


def key_terms(keys, rates, up, down, mid, end):
    norm = lax.rsqrt(jnp.sum(keys * keys, -1, keepdims=True) + 1e-6)
    unit = keys * norm
    write = unit * rates * up
    low = unit * down
    return (write.astype(BF16), low.astype(BF16), (write * mid).astype(BF16)) + split(low * end)


def iota(shape, dim):
    return lax.broadcasted_iota(jnp.int32, shape, dim)


def tails_kernel(width, *refs):
    ins, out_ref, held, sems = refs[:3], refs[3], refs[4], refs[5]
    rows = ins[0].shape[0]
    copies = [
        pltpu.make_async_copy(ref.at[pl.ds(rows - EDGE, EDGE)], held.at[n], sems.at[n]) for n, ref in enumerate(ins)
    ]
    for copy in copies:
        copy.start()
    parts = []
    for n, copy in enumerate(copies):
        copy.wait()
        parts.append(held[n].astype(F32)[EDGE - width :])
    parts.append(jnp.zeros((EDGE - 3 * width, out_ref.shape[1]), F32))
    out_ref[...] = jnp.concatenate(parts, 0).astype(BF16)


def prepare_kernel(
    groups, g_ref, k_ref, v_ref, beta_ref, taps_ref,
    write_ref, low_ref, kin_ref, khi_ref, klo_ref, vb_ref, up_ref, down_ref, marks_ref, edge_ref, rates_ref,
):
    rows, width = g_ref.shape
    cols = width // groups
    heads = cols // D
    middle = rows // 2 - 1
    at, other = iota((rows, rows), 0), iota((rows, rows), 1)
    plus = jnp.where((other <= at) & (other > middle), 1.0, 0.0)
    minus = jnp.where((other > at) & (other <= middle), 1.0, 0.0)
    summing = (plus - minus).astype(BF16)
    rates = beta_ref[...].astype(F32).T
    rates_ref[...] = rates[:EDGE]
    lane = iota(rates.shape, 1)
    for i in range(groups):
        whole = slice(i * cols, (i + 1) * cols)
        sums = dot(summing, g_ref[:, whole])
        up = jnp.exp(sums)
        down = jnp.exp(-sums)
        up_ref[:, whole] = up
        down_ref[:, whole] = down[:EDGE]
        mid = jnp.exp(g_ref[0:EDGE, whole].astype(F32)[0:1] - sums[0:1])
        end = up[rows - 1 : rows]
        marks_ref[:, whole] = jnp.concatenate([mid, end] * 4, 0)
        edge_ref[0, :, whole] = k_ref[0:EDGE, whole]
        keys = conv(k_ref[:, whole].astype(F32), taps_ref[1, :, whole])
        for h in range(heads):
            c = slice(h * D, (h + 1) * D)
            to = slice((i * heads + h) * D, (i * heads + h + 1) * D)
            rate = jnp.sum(jnp.where(lane == i * heads + h, rates, 0.0), -1, keepdims=True)
            out = key_terms(keys[:, c], rate, up[:, c], down[:, c], mid[:, c], end[:, c])
            for ref, value in zip((write_ref, low_ref, kin_ref, khi_ref, klo_ref), out):
                ref[:, to] = value
        edge_ref[1, :, whole] = v_ref[0:EDGE, whole]
        values = conv(v_ref[:, whole].astype(F32), taps_ref[2, :, whole])
        for h in range(heads):
            to = slice((i * heads + h) * D, (i * heads + h + 1) * D)
            rate = jnp.sum(jnp.where(lane == i * heads + h, rates, 0.0), -1, keepdims=True)
            vb_ref[:, to] = (values[:, h * D : (h + 1) * D] * rate).astype(BF16)


def edge_rows(rim, which, raw, taps):
    width = taps.shape[0]
    first = which * (width - 1)
    before = pltpu.roll(rim, (8 - (width - 1) - first) % rim.shape[0], 0)[0:8]
    return conv(jnp.concatenate([before, raw.astype(F32)], 0), taps)[8:]


def solve_heads(lows, rows):
    lane_sub = iota((SUB, rows), 1)
    blocks = rows // SUB
    at, other = iota((rows, rows), 0), iota((rows, rows), 1)
    same = (at // SUB) == (other // SUB)
    packed = []
    for low in lows:
        own = jnp.where(same, low, 0.0)
        total = own[0:SUB]
        for b in range(1, blocks):
            total = total + own[b * SUB : (b + 1) * SUB]
        packed.append(total)
    unit = jnp.where(lane_sub % SUB == iota((SUB, rows), 0), 1.0, 0.0)
    solved = [unit for _ in lows]
    group_start = lane_sub - lane_sub % SUB
    for j in range(SUB - 1):
        for n, total in enumerate(packed):
            spread = jnp.take_along_axis(total, group_start + j, axis=1, mode="promise_in_bounds")
            solved[n] = solved[n] - spread * solved[n][j : j + 1]
    full = [jnp.where(same, jnp.concatenate([x] * blocks, 0), 0.0) for x in solved]
    size = SUB
    while size < rows:
        mask = (at // (2 * size) == other // (2 * size)) & (at // size != other // size)
        lower = [slice(p * size, (p + 1) * size) for p in range(1, rows // size, 2)]
        take = lambda x: jnp.concatenate([x[s] for s in lower], 0)
        small_mask = take(mask)
        parts = [split(x) for x in full]
        links = []
        for low in lows:
            masked = jnp.where(small_mask, take(low), 0.0)
            total = masked[:size]
            for p in range(1, rows // (2 * size)):
                total = total + masked[p * size : (p + 1) * size]
            links.append(split(total))
        inner = [dot3(link, part) for link, part in zip(links, parts)]
        zeros = jnp.zeros((size, rows), F32)
        spread = []
        for x in inner:
            pieces = []
            for p in range(rows // (2 * size)):
                own = jnp.where(iota((size, rows), 1) // (2 * size) == p, x, 0.0) if 2 * size < rows else x
                pieces += [zeros, own]
            spread.append(split(jnp.concatenate(pieces, 0)))
        fixes = [dot3((take(part[0]), take(part[1])), s) for part, s in zip(parts, spread)]
        result = []
        for x, fix in zip(full, fixes):
            pieces = []
            for p in range(rows // (2 * size)):
                pieces += [
                    x[2 * p * size : (2 * p + 1) * size],
                    x[(2 * p + 1) * size : (2 * p + 2) * size] - fix[p * size : (p + 1) * size],
                ]
            result.append(jnp.concatenate(pieces, 0))
        full = result
        size *= 2
    return full


def block_kernel(
    group_ref, later_ref, rim_ref, edge_ref, rates_ref, taps_ref, up_ref, down_ref, marks_ref,
    write_ref, low_ref, kin_ref, khi_ref, klo_ref, vb_ref,
    move_ref, made_ref, low_out_ref,
):
    rows = low_ref.shape[0]
    heads = move_ref.shape[0]
    cols = heads * D
    start = pl.multiple_of(group_ref[0] * cols, cols)
    mine = pl.ds(start, cols)
    rim = jnp.where(later_ref[0] > 0, rim_ref[:, mine].astype(F32), 0.0)
    keys = edge_rows(rim, 1, edge_ref[0, :, mine], taps_ref[1, :, mine])
    values = edge_rows(rim, 2, edge_ref[1, :, mine], taps_ref[2, :, mine])
    up, down, marks = up_ref[0:EDGE, mine], down_ref[:, mine], marks_ref[:, mine]
    rates = rates_ref[...]
    lane = iota(rates.shape, 1)
    base = group_ref[0] * heads
    at, other = iota((rows, rows), 0), iota((rows, rows), 1)
    lows, ends, sides = [], [], []
    for h in range(heads):
        c = slice(h * D, (h + 1) * D)
        here = pl.ds(pl.multiple_of(start + h * D, D), D)
        rate = jnp.sum(jnp.where(lane == base + h, rates, 0.0), -1, keepdims=True)
        edge = key_terms(keys[:, c], rate, up[:, c], down[:, c], marks[0:1, c], marks[1:2, c])
        write, low, kin, khi, klo = [
            jnp.concatenate([e, ref[EDGE:, here]], 0)
            for e, ref in zip(edge, (write_ref, low_ref, kin_ref, khi_ref, klo_ref))
        ]
        vb = jnp.concatenate([(values[:, c] * rate).astype(BF16), vb_ref[EDGE:, here]], 0)
        low_out_ref[:, c] = low
        lows.append(jnp.where(at > other, dot_t(write, low), 0.0))
        ends.append((khi, klo))
        sides.append(jnp.concatenate([kin, vb], 1))
    solved = solve_heads(lows, rows)
    made = []
    for t, side in zip(solved, sides):
        both = dot(jnp.concatenate(split(t), 0), side)
        made.append((both[:rows] + both[rows:]).astype(BF16))
    for h in range(heads):
        c = slice(h * D, (h + 1) * D)
        sums = t_dot(ends[h][0], made[h]) + t_dot(ends[h][1], made[h])
        fade = marks[0:1, c] * marks[1:2, c] - 1.0
        move = jnp.where(at == other, fade, 0.0) - sums[:, :D]
        made_ref[h] = made[h]
        move_ref[h, :, :D] = move.astype(BF16)
        move_ref[h, :, D:] = sums[:, D:].astype(BF16)


def local_kernel(count, later_ref, *refs):
    group_refs, refs = refs[:count], refs[count:]
    rim_ref, q_ref, gate_ref, taps_ref, gain_ref, up_ref, marks_ref, *refs = refs
    ins, outs, held, sems = refs[: 2 * count], refs[2 * count : 5 * count], refs[-2], refs[-1]
    rows, cols = outs[0].shape
    heads = cols // D
    starts = [pl.multiple_of(group_refs[i][0] * cols, cols) for i in range(count)]
    copies = {}
    for i in range(count):
        for n, ref in enumerate((q_ref, gate_ref)):
            copies[n, i] = pltpu.make_async_copy(ref.at[:, pl.ds(starts[i], cols)], held.at[n, i], sems.at[n, i])
            copies[n, i].start()
    at, other = iota((rows, rows), 0), iota((rows, rows), 1)
    for i in range(count):
        low_ref, made_ref = ins[2 * i : 2 * i + 2]
        reach_ref, own_ref, scale_ref = outs[3 * i : 3 * i + 3]
        mine = pl.ds(starts[i], cols)
        taps = taps_ref[0, :, mine]
        rim = jnp.where(later_ref[0] > 0, rim_ref[:, mine].astype(F32), 0.0)
        mid = marks_ref[0:1, mine]
        copies[0, i].wait()
        edge = edge_rows(rim, 0, held[0, i, 0:EDGE], taps)
        queries = jnp.concatenate([edge, conv(held[0, i].astype(F32), taps)[EDGE:]], 0) * up_ref[:, mine]
        copies[1, i].wait()
        gate = held[1, i].astype(F32)
        for h in range(heads):
            c = slice(h * D, (h + 1) * D)
            scores = jnp.where(at >= other, dot_t(queries[:, c].astype(BF16), low_ref[:, c]), 0.0)
            both = dot(jnp.concatenate(split(scores), 0), made_ref[h])
            seen = both[:rows] + both[rows:]
            reach_ref[:, c] = (queries[:, c] * mid[:, c] - seen[:, :D]).astype(BF16)
            own_ref[:, c] = seen[:, D:]
            scale_ref[:, c] = gain_ref[...] * (0.5 + 0.5 * jnp.tanh(0.5 * gate[:, c]))


def follow(move, add, ahead):
    return (ahead.astype(F32) + add.astype(F32) + dot(move, ahead)).astype(BF16)


def follow_pair(pair, ahead):
    return follow(pair[:, :D], pair, ahead)


def chain_kernel(me_ref, *refs):
    pairs, move_ref, add_ref = refs[:-2], refs[-2], refs[-1]
    heads = move_ref.shape[0]
    for m in range(len(pairs)):

        @pl.when(me_ref[0] == m)
        def _():
            steps = [[pairs[m ^ b][h] for h in range(heads)] for b in range(len(pairs))]
            while len(steps) > 1:
                steps = [
                    [follow_pair(steps[b + 1][h], steps[b][h]) for h in range(heads)] for b in range(0, len(steps), 2)
                ]
            for h in range(heads):
                move_ref[h] = steps[0][h][:, :D]
                add_ref[h] = steps[0][h][:, D:]


def prefix_kernel(me_ref, *refs):
    pairs, before_ref = refs[:-1], refs[-1]
    heads = before_ref.shape[1]
    for m in range(len(pairs)):

        @pl.when(me_ref[0] == m)
        def _():
            now = [pairs[m][h] for h in range(heads)]
            for b in range(len(pairs) - 1):
                for h in range(heads):
                    if b:
                        now[h] = follow_pair(pairs[m ^ b][h], now[h])
                    before_ref[b, h] = now[h]


def absorb_kernel(count, wide, sends, which_ref, *refs):
    parts, refs = refs[:count], refs[count:]
    if sends:
        own_move, own_add, refs = refs[0], refs[1], refs[2:]
    have, outs = (refs[:2], refs[2:]) if wide else (None, refs)
    heads = parts[0].shape[0]
    for d in range(-1, count):

        @pl.when(which_ref[0] == d)
        def _():
            for h in range(heads):
                if d < 0:
                    ahead = have[1][h] if wide else jnp.zeros(parts[0].shape[1:], BF16)
                else:
                    ahead = follow(have[0][h], have[1][h], parts[d][h]) if wide else parts[d][h]
                outs[0][h] = ahead
                if sends:
                    outs[1][h] = follow(own_move[h], own_add[h], ahead)


def absorb_four_kernel(span_ref, move_ref, add_ref, came_ref, ahead_ref, state_ref, mixed_ref):
    for upper in (0, 1):

        @pl.when(span_ref[0] & 1 == upper)
        def _():
            for h in range(add_ref.shape[0]):
                ahead = came_ref[h] if upper else jnp.zeros(came_ref.shape[1:], BF16)
                state = follow(move_ref[h], add_ref[h], ahead) if upper else add_ref[h]
                ahead_ref[h] = ahead
                state_ref[h] = state
                mixed_ref[h] = state if upper else move_ref[h]


def starts_four_kernel(me_ref, span_ref, ahead_ref, near_ref, far_ref, before_ref, *outs):
    heads = ahead_ref.shape[0]

    def state_ahead(h):
        both = follow(near_ref[h], ahead_ref[h], far_ref[h])
        state = jnp.where(span_ref[0] == 3, both.astype(F32), ahead_ref[h].astype(F32))
        return jnp.where(span_ref[0] == 2, near_ref[h].astype(F32), state).astype(BF16)

    give_starts(me_ref, before_ref, [state_ahead(h) for h in range(heads)], outs)


def give_starts(me_ref, before_ref, first, outs):
    heads = len(first)
    later = [
        [follow(before_ref[b, h, :, :D], before_ref[b, h, :, D:], first[h]) for h in range(heads)]
        for b in range(len(outs) - 1)
    ]
    for m in range(len(outs)):

        @pl.when(me_ref[0] == m)
        def _():
            for b in range(len(outs)):
                for h in range(heads):
                    outs[m ^ b][h] = later[b - 1][h] if b else first[h]


def starts_kernel(count, me_ref, which_ref, *refs):
    parts, (move_ref, add_ref, before_ref, *outs) = refs[:count], refs[count:]
    heads = move_ref.shape[0]

    def state_ahead(h):
        came = jnp.zeros(move_ref.shape[1:], F32)
        for d in range(count):
            came = jnp.where(which_ref[0] == d, parts[d][h].astype(F32), came)
        return follow(move_ref[h], add_ref[h], came.astype(BF16))

    give_starts(me_ref, before_ref, [state_ahead(h) for h in range(heads)], outs)


def finish_kernel(count, more, *refs):
    groups, refs = refs[:count], refs[count:]
    refs = refs[1:] if more else refs
    reach, own, scale, starts = (refs[k * count : (k + 1) * count] for k in range(4))
    out_ref, held, sems = refs[4 * count :]
    heads = starts[0].shape[0]
    cols = heads * D
    copies = []
    for n in range(count):
        for h in range(heads):
            c = slice(h * D, (h + 1) * D)
            found = own[n][:, c] + dot(reach[n][:, c], starts[n][h])
            found = found.astype(BF16).astype(F32)
            mean = jnp.mean(found * found, -1, keepdims=True)
            held[n, :, c] = (found * lax.rsqrt(mean + 1e-5) * scale[n][:, c]).astype(BF16)
        to = pl.ds(pl.multiple_of(groups[n][0] * cols, cols), cols)
        copies.append(pltpu.make_async_copy(held.at[n], out_ref.at[:, to], sems.at[n]))
        copies[n].start()
    for copy in copies:
        copy.wait()


def whole_route(pairs, count):
    sources = [i for i in range(count) if i not in [a for a, _ in pairs]]
    targets = [i for i in range(count) if i not in [b for _, b in pairs]]
    if len(sources) <= 5:
        cost = lambda order: sum(abs(a - b) if a != b else count * count for a, b in zip(sources, order))
        targets = min(itertools.permutations(targets), key=cost)
    return pairs + list(zip(sources, targets))


def params():
    return pltpu.CompilerParams(vmem_limit_bytes=VMEM_LIMIT)


def shards(query_raw, key_raw, value_raw, log_decay, beta, conv_weight, out_gate, norm_gain):
    rows, width = query_raw.shape
    groups = lax.axis_size("head")
    spans = lax.axis_size("ctx")
    cols = width // groups
    heads = cols // D
    rim_width = conv_weight.shape[1] - 1
    me = lax.axis_index("head").astype(jnp.int32).reshape(1)
    span = lax.axis_index("ctx").astype(jnp.int32).reshape(1)
    group_ids = [me ^ j for j in range(groups)]
    later = (me + span > 0).astype(jnp.int32)
    rounds = (spans - 1).bit_length()
    places = [jnp.where((span >> r) & 1 > 0, span & ((1 << r) - 1), -1) for r in range(rounds)]
    (group_ids, later, places, span), query_raw, key_raw, value_raw, log_decay = lax.optimization_barrier(
        ((group_ids, later, places, span), query_raw, key_raw, value_raw, log_decay)
    )
    me_arg = group_ids[0]
    near = [pltpu.with_memory_space_constraint(x, pltpu.VMEM) for x in (log_decay, key_raw, value_raw)]
    query_raw, key_raw, value_raw, log_decay, out_gate = (
        pltpu.with_memory_space_constraint(x, pltpu.HBM) for x in (query_raw, key_raw, value_raw, log_decay, out_gate)
    )
    beta = beta.T

    smem = pl.BlockSpec(memory_space=pltpu.SMEM)
    vmem = pl.BlockSpec(memory_space=pltpu.VMEM)
    far = pl.BlockSpec(memory_space=pl.ANY)

    tails = pl.pallas_call(
        functools.partial(tails_kernel, rim_width),
        in_specs=[far] * 3,
        out_specs=vmem,
        out_shape=jax.ShapeDtypeStruct((EDGE, width), BF16),
        scratch_shapes=[pltpu.VMEM((3, EDGE, width), BF16), pltpu.SemaphoreType.DMA((3,))],
        compiler_params=params(),
        name="tails",
    )(query_raw, key_raw, value_raw)
    total = groups * spans
    rim = lax.ppermute(tails, ("ctx", "head"), [(i, (i + 1) % total) for i in range(total)])

    wide16 = jax.ShapeDtypeStruct((rows, width), BF16)
    prepared = pl.pallas_call(
        functools.partial(prepare_kernel, groups),
        in_specs=[vmem] * 5,
        out_specs=[vmem] * 11,
        out_shape=[wide16] * 6
        + [
            jax.ShapeDtypeStruct((rows, width), F32),
            jax.ShapeDtypeStruct((EDGE, width), F32),
            jax.ShapeDtypeStruct((8, width), F32),
            jax.ShapeDtypeStruct((2, EDGE, width), BF16),
            jax.ShapeDtypeStruct((EDGE, beta.shape[0]), F32),
        ],
        compiler_params=params(),
        cost_estimate=pl.CostEstimate(flops=20_000_000, bytes_accessed=9_000_000, transcendentals=2_000_000),
        name="prepare",
    )(*near, beta, conv_weight)
    write, low, kin, khi, klo, vb, up, down, marks, edges, rates = prepared

    moves, made, lows = [None] * groups, [None] * groups, [None] * groups
    order = list(range(groups - 1, -1, -1))
    for j in order:
        moves[j], made[j], lows[j] = pl.pallas_call(
            block_kernel,
            in_specs=[smem] * 2 + [vmem] * 13,
            out_specs=[vmem] * 3,
            out_shape=[
                jax.ShapeDtypeStruct((heads, D, 2 * D), BF16),
                jax.ShapeDtypeStruct((heads, rows, 2 * D), BF16),
                jax.ShapeDtypeStruct((rows, cols), BF16),
            ],
            compiler_params=params(),
            name="block",
        )(group_ids[j], later, rim, edges, rates, conv_weight, up, down, marks, write, low, kin, khi, klo, vb)

    def call(kernel, name, in_specs, outs, scratch=()):
        return pl.pallas_call(
            kernel,
            in_specs=in_specs,
            out_specs=[vmem] * len(outs),
            out_shape=[jax.ShapeDtypeStruct(*out) for out in outs],
            scratch_shapes=scratch,
            compiler_params=params(),
            name=name,
        )

    def swap(array, j, axis="head"):
        return lax.ppermute(array, axis, [(i, i ^ j) for i in range(lax.axis_size(axis))])

    block16, block32 = ((rows, cols), BF16), ((rows, cols), F32)
    state, pair = ((heads, D, D), BF16), ((heads, D, 2 * D), BF16)

    def local(js):
        if not js:
            return {}
        got = call(
            functools.partial(local_kernel, len(js)),
            "local",
            [smem] * (1 + len(js)) + [vmem, far, far] + [vmem] * (4 + 2 * len(js)),
            [block16, block32, block32] * len(js),
            [pltpu.VMEM((2, len(js), rows, cols), BF16), pltpu.SemaphoreType.DMA((2, len(js)))],
        )(
            later, *[group_ids[j] for j in js], rim, query_raw, out_gate, conv_weight, norm_gain.reshape(1, D),
            up, marks, *[x for j in js for x in (lows[j], made[j])],
        )
        return {j: got[3 * i : 3 * i + 3] for i, j in enumerate(js)}

    came_pairs = [swap(moves[j], j) if j else moves[j] for j in range(groups)]
    left = list(range(groups))
    came_pairs, found = lax.optimization_barrier((came_pairs, local(left[: groups // 2])))
    left = left[groups // 2 :]
    move, add = call(chain_kernel, "chain", [smem] + [vmem] * groups, [state] * 2)(me_arg, *came_pairs)

    def tell(array, r):
        half = 1 << r
        routes = [
            [(low + half - 1, low + half + d) for low in range(0, spans, 2 * half) if low + half + d < spans]
            for d in range(half)
        ]
        return [lax.ppermute(array, "ctx", whole_route(route, spans)) for route in routes if route]

    def absorb(r, parts, own, have):
        wide, sends = have is not None, own is not None
        return call(
            functools.partial(absorb_kernel, len(parts), wide, sends),
            "absorb",
            [smem] + [vmem] * (len(parts) + 2 * wide + 2 * sends),
            [state] * (1 + sends),
        )(places[r], *parts, *(own or ()), *(have or ()))

    adds = tell(add, 0) if rounds else []
    ahead, send_move = None, move
    if spans == 4:
        ahead, told, mixed = call(absorb_four_kernel, "absorb", [smem] + [vmem] * 3, [state] * 3)(
            span, move, add, adds[0]
        )
        adds = [
            lax.ppermute(mixed, "ctx", whole_route([(0, 1), (1, 2), (2, 3)], 4)),
            lax.ppermute(told, "ctx", [(1, 3), (3, 2), (2, 1), (0, 0)]),
        ]
    for r in range(rounds - 1 if spans != 4 else 0):
        moves_in = tell(send_move, r)
        got_add = absorb(r, adds, (move, add), ahead)
        adds = tell(got_add[1], r + 1)
        more = r + 2 < rounds
        got_move = absorb(r, moves_in, (move, move) if more else None, (ahead[0], ahead[0]) if ahead else None)
        ahead = (got_move[0], got_add[0])
        send_move = got_move[1] if more else None
    (before,) = call(
        prefix_kernel, "prefix", [smem] + [vmem] * groups, [((groups - 1, heads, D, 2 * D), BF16)]
    )(me_arg, *came_pairs)
    adds, before, mine = lax.optimization_barrier((adds, before, local(left)))
    found.update(mine)
    if spans == 4:
        starts = call(starts_four_kernel, "starts", [smem] * 2 + [vmem] * 4, [state] * groups)(
            me_arg, span, ahead, *adds, before
        )
    else:
        ahead = (jnp.zeros(*state),) * 2 if ahead is None else ahead
        starts = call(
            functools.partial(starts_kernel, len(adds)),
            "starts",
            [smem] * 2 + [vmem] * (len(adds) + 3),
            [state] * groups,
        )(me_arg, places[-1] if rounds else later, *adds, *ahead, before)
    starts = [starts[0]] + [swap(starts[j], j) for j in range(1, groups)]

    def finish(js, out):
        more = out is not None
        return pl.pallas_call(
            functools.partial(finish_kernel, len(js), more),
            in_specs=[smem] * len(js) + [far] * more + [vmem] * (4 * len(js)),
            out_specs=far,
            out_shape=jax.ShapeDtypeStruct((rows, width), BF16),
            scratch_shapes=[pltpu.VMEM((len(js), rows, cols), BF16), pltpu.SemaphoreType.DMA((len(js),))],
            input_output_aliases={len(js): 0} if more else {},
            compiler_params=params(),
            name="finish",
        )(
            *[group_ids[j] for j in js], *([out] if more else []),
            *[found[j][k] for k in range(3) for j in js], *[starts[j] for j in js],
        )

    first = [j for j in (0, FIRST) if j < groups]
    rest = [j for j in range(groups) if j not in first]
    out = finish(first, None)
    return finish(rest, out) if rest else out


def solution(mesh):
    tokens = P(("dp", "ctx", "head"), None)
    placed = (tokens, tokens, tokens, tokens, tokens, P(), tokens, P())
    return jax.shard_map(shards, mesh=mesh, in_specs=placed, out_specs=tokens, check_vma=False)
```

```python
import functools
import itertools

import jax
import jax.numpy as jnp
from jax import lax
from jax.experimental import pallas as pl
from jax.experimental.pallas import tpu as pltpu
from jax.sharding import PartitionSpec as P

D = 128
SUB = 16
EDGE = 16
F32 = jnp.float32
BF16 = jnp.bfloat16
FIRST = 1
VMEM_LIMIT = 32 * 1024 * 1024


def dot(a, b):
    return jnp.dot(a, b, preferred_element_type=F32)


def dot_t(a, b):
    return lax.dot_general(a, b, (((1,), (1,)), ((), ())), preferred_element_type=F32)


def t_dot(a, b):
    return lax.dot_general(a, b, (((0,), (0,)), ((), ())), preferred_element_type=F32)


def split(x):
    hi = x.astype(BF16)
    return hi, (x - hi.astype(F32)).astype(BF16)


def dot3(a, b):
    a_hi, a_lo = a
    b_hi, b_lo = b
    rows = a_hi.shape[0]
    both = dot(jnp.concatenate([a_hi, a_lo], 0), b_hi)
    return both[:rows] + both[rows:] + dot(a_hi, b_lo)


def silu(u):
    half = 0.5 * u
    return half + half * jnp.tanh(half)


def conv(x, taps):
    width = taps.shape[0]
    total = x * taps[width - 1 : width]
    for back in range(1, width):
        total = total + pltpu.roll(x, back, 0) * taps[width - 1 - back : width - back]
    return silu(total).astype(BF16).astype(F32)


def key_terms(keys, rates, up, down, mid, end):
    norm = lax.rsqrt(jnp.sum(keys * keys, -1, keepdims=True) + 1e-6)
    unit = keys * norm
    write = unit * rates * up
    low = unit * down
    return (write.astype(BF16), low.astype(BF16), (write * mid).astype(BF16)) + split(low * end)


def iota(shape, dim):
    return lax.broadcasted_iota(jnp.int32, shape, dim)


def tails_kernel(width, *refs):
    ins, out_ref, held, sems = refs[:3], refs[3], refs[4], refs[5]
    rows = ins[0].shape[0]
    copies = [
        pltpu.make_async_copy(ref.at[pl.ds(rows - EDGE, EDGE)], held.at[n], sems.at[n]) for n, ref in enumerate(ins)
    ]
    for copy in copies:
        copy.start()
    parts = []
    for n, copy in enumerate(copies):
        copy.wait()
        parts.append(held[n].astype(F32)[EDGE - width :])
    parts.append(jnp.zeros((EDGE - 3 * width, out_ref.shape[1]), F32))
    out_ref[...] = jnp.concatenate(parts, 0).astype(BF16)


def prepare_kernel(
    groups, g_ref, k_ref, v_ref, beta_ref, taps_ref,
    write_ref, low_ref, kin_ref, khi_ref, klo_ref, vb_ref, up_ref, down_ref, marks_ref, edge_ref, rates_ref,
    held, sem,
):
    rows, width = g_ref.shape
    copy = pltpu.make_async_copy(g_ref, held, sem)
    copy.start()
    cols = width // groups
    heads = cols // D
    middle = rows // 2 - 1
    at, other = iota((rows, rows), 0), iota((rows, rows), 1)
    plus = jnp.where((other <= at) & (other > middle), 1.0, 0.0)
    minus = jnp.where((other > at) & (other <= middle), 1.0, 0.0)
    summing = (plus - minus).astype(BF16)
    rates = beta_ref[...].astype(F32).T
    rates_ref[...] = rates[:EDGE]
    lane = iota(rates.shape, 1)
    for i in range(groups):
        whole = slice(i * cols, (i + 1) * cols)
        edge_ref[0, :, whole] = k_ref[0:EDGE, whole]
        edge_ref[1, :, whole] = v_ref[0:EDGE, whole]
        values = conv(v_ref[:, whole].astype(F32), taps_ref[2, :, whole])
        for h in range(heads):
            to = slice((i * heads + h) * D, (i * heads + h + 1) * D)
            rate = jnp.sum(jnp.where(lane == i * heads + h, rates, 0.0), -1, keepdims=True)
            vb_ref[:, to] = (values[:, h * D : (h + 1) * D] * rate).astype(BF16)
    copy.wait()
    for i in range(groups):
        whole = slice(i * cols, (i + 1) * cols)
        sums = dot(summing, held[:, whole])
        up = jnp.exp(sums)
        down = jnp.exp(-sums)
        up_ref[:, whole] = up
        down_ref[:, whole] = down[:EDGE]
        mid = jnp.exp(held[0:EDGE, whole].astype(F32)[0:1] - sums[0:1])
        end = up[rows - 1 : rows]
        marks_ref[:, whole] = jnp.concatenate([mid, end] * 4, 0)
        keys = conv(k_ref[:, whole].astype(F32), taps_ref[1, :, whole])
        for h in range(heads):
            c = slice(h * D, (h + 1) * D)
            to = slice((i * heads + h) * D, (i * heads + h + 1) * D)
            rate = jnp.sum(jnp.where(lane == i * heads + h, rates, 0.0), -1, keepdims=True)
            out = key_terms(keys[:, c], rate, up[:, c], down[:, c], mid[:, c], end[:, c])
            for ref, value in zip((write_ref, low_ref, kin_ref, khi_ref, klo_ref), out):
                ref[:, to] = value


def edge_rows(rim, which, raw, taps):
    width = taps.shape[0]
    first = which * (width - 1)
    before = pltpu.roll(rim, (8 - (width - 1) - first) % rim.shape[0], 0)[0:8]
    return conv(jnp.concatenate([before, raw.astype(F32)], 0), taps)[8:]


def solve_heads(lows, rows):
    lane_sub = iota((SUB, rows), 1)
    blocks = rows // SUB
    at, other = iota((rows, rows), 0), iota((rows, rows), 1)
    same = (at // SUB) == (other // SUB)
    packed = []
    for low in lows:
        own = jnp.where(same, low, 0.0)
        total = own[0:SUB]
        for b in range(1, blocks):
            total = total + own[b * SUB : (b + 1) * SUB]
        packed.append(total)
    half = SUB // 2
    unit = jnp.where(lane_sub % SUB == iota((SUB, rows), 0), 1.0, 0.0)
    solved = [[unit[:half], unit[half:]] for _ in lows]
    group_start = (lane_sub - lane_sub % SUB)[:half]
    for j in range(SUB - 1):
        for n, total in enumerate(packed):
            row = solved[n][j // half][j % half : j % half + 1]
            for part in range((j + 1) // half, 2):
                rows_here = total[part * half : (part + 1) * half]
                spread = jnp.take_along_axis(rows_here, group_start + j, axis=1, mode="promise_in_bounds")
                solved[n][part] = solved[n][part] - spread * row
    solved = [jnp.concatenate(parts, 0) for parts in solved]
    full = [jnp.where(same, jnp.concatenate([x] * blocks, 0), 0.0) for x in solved]
    size = SUB
    while size < rows:
        mask = (at // (2 * size) == other // (2 * size)) & (at // size != other // size)
        lower = [slice(p * size, (p + 1) * size) for p in range(1, rows // size, 2)]
        take = lambda x: jnp.concatenate([x[s] for s in lower], 0)
        small_mask = take(mask)
        parts = [split(x) for x in full]
        links = []
        for low in lows:
            masked = jnp.where(small_mask, take(low), 0.0)
            total = masked[:size]
            for p in range(1, rows // (2 * size)):
                total = total + masked[p * size : (p + 1) * size]
            links.append(split(total))
        inner = [dot3(link, part) for link, part in zip(links, parts)]
        zeros = jnp.zeros((size, rows), F32)
        spread = []
        for x in inner:
            pieces = []
            for p in range(rows // (2 * size)):
                own = jnp.where(iota((size, rows), 1) // (2 * size) == p, x, 0.0) if 2 * size < rows else x
                pieces += [zeros, own]
            spread.append(split(jnp.concatenate(pieces, 0)))
        fixes = [dot3((take(part[0]), take(part[1])), s) for part, s in zip(parts, spread)]
        result = []
        for x, fix in zip(full, fixes):
            pieces = []
            for p in range(rows // (2 * size)):
                pieces += [
                    x[2 * p * size : (2 * p + 1) * size],
                    x[(2 * p + 1) * size : (2 * p + 2) * size] - fix[p * size : (p + 1) * size],
                ]
            result.append(jnp.concatenate(pieces, 0))
        full = result
        size *= 2
    return full


def block_kernel(count, later_ref, *refs):
    group_refs, refs = refs[:count], refs[count:]
    rim_ref, edge_ref, rates_ref, taps_ref, up_ref, down_ref, marks_ref, *refs = refs
    write_ref, low_ref, kin_ref, khi_ref, klo_ref, vb_ref, *outs = refs
    rows = low_ref.shape[0]
    heads = outs[0].shape[0]
    cols = heads * D
    rates = rates_ref[...]
    lane = iota(rates.shape, 1)
    at, other = iota((rows, rows), 0), iota((rows, rows), 1)
    lows, ends, sides, fades = [], [], [], []
    for n in range(count):
        start = pl.multiple_of(group_refs[n][0] * cols, cols)
        mine = pl.ds(start, cols)
        rim = jnp.where(later_ref[0] > 0, rim_ref[:, mine].astype(F32), 0.0)
        keys = edge_rows(rim, 1, edge_ref[0, :, mine], taps_ref[1, :, mine])
        values = edge_rows(rim, 2, edge_ref[1, :, mine], taps_ref[2, :, mine])
        up, down, marks = up_ref[0:EDGE, mine], down_ref[:, mine], marks_ref[:, mine]
        for h in range(heads):
            c = slice(h * D, (h + 1) * D)
            here = pl.ds(pl.multiple_of(start + h * D, D), D)
            rate = jnp.sum(jnp.where(lane == group_refs[n][0] * heads + h, rates, 0.0), -1, keepdims=True)
            edge = key_terms(keys[:, c], rate, up[:, c], down[:, c], marks[0:1, c], marks[1:2, c])
            write, low, kin, khi, klo = [
                jnp.concatenate([e, ref[EDGE:, here]], 0)
                for e, ref in zip(edge, (write_ref, low_ref, kin_ref, khi_ref, klo_ref))
            ]
            vb = jnp.concatenate([(values[:, c] * rate).astype(BF16), vb_ref[EDGE:, here]], 0)
            outs[3 * n + 2][:, c] = low
            lows.append(jnp.where(at > other, dot_t(write, low), 0.0))
            ends.append((khi, klo))
            sides.append(jnp.concatenate([kin, vb], 1))
            fades.append(marks[0:1, c] * marks[1:2, c] - 1.0)
    solved = solve_heads(lows, rows)
    made = []
    for t, side in zip(solved, sides):
        both = dot(jnp.concatenate(split(t), 0), side)
        made.append((both[:rows] + both[rows:]).astype(BF16))
    for k, fade in enumerate(fades):
        n, h = divmod(k, heads)
        sums = t_dot(ends[k][0], made[k]) + t_dot(ends[k][1], made[k])
        move = jnp.where(at == other, fade, 0.0) - sums[:, :D]
        outs[3 * n + 1][h] = made[k]
        outs[3 * n][h, :, :D] = move.astype(BF16)
        outs[3 * n][h, :, D:] = sums[:, D:].astype(BF16)


def local_kernel(count, later_ref, *refs):
    group_refs, refs = refs[:count], refs[count:]
    rim_ref, q_ref, gate_ref, taps_ref, gain_ref, up_ref, marks_ref, *refs = refs
    ins, outs, held, sems = refs[: 2 * count], refs[2 * count : 5 * count], refs[-2], refs[-1]
    rows, cols = outs[0].shape
    heads = cols // D
    starts = [pl.multiple_of(group_refs[i][0] * cols, cols) for i in range(count)]
    copies = {}
    for i in range(count):
        for n, ref in enumerate((q_ref, gate_ref)):
            copies[n, i] = pltpu.make_async_copy(ref.at[:, pl.ds(starts[i], cols)], held.at[n, i], sems.at[n, i])
            copies[n, i].start()
    at, other = iota((rows, rows), 0), iota((rows, rows), 1)
    for i in range(count):
        low_ref, made_ref = ins[2 * i : 2 * i + 2]
        reach_ref, own_ref, scale_ref = outs[3 * i : 3 * i + 3]
        mine = pl.ds(starts[i], cols)
        taps = taps_ref[0, :, mine]
        rim = jnp.where(later_ref[0] > 0, rim_ref[:, mine].astype(F32), 0.0)
        mid = marks_ref[0:1, mine]
        copies[0, i].wait()
        edge = edge_rows(rim, 0, held[0, i, 0:EDGE], taps)
        queries = jnp.concatenate([edge, conv(held[0, i].astype(F32), taps)[EDGE:]], 0) * up_ref[:, mine]
        copies[1, i].wait()
        gate = held[1, i].astype(F32)
        for h in range(heads):
            c = slice(h * D, (h + 1) * D)
            scores = jnp.where(at >= other, dot_t(queries[:, c].astype(BF16), low_ref[:, c]), 0.0)
            both = dot(jnp.concatenate(split(scores), 0), made_ref[h])
            seen = both[:rows] + both[rows:]
            reach_ref[:, c] = (queries[:, c] * mid[:, c] - seen[:, :D]).astype(BF16)
            own_ref[:, c] = seen[:, D:]
            scale_ref[:, c] = gain_ref[...] * (0.5 + 0.5 * jnp.tanh(0.5 * gate[:, c]))


def follow(move, add, ahead):
    return (ahead.astype(F32) + add.astype(F32) + dot(move, ahead)).astype(BF16)


def follow_pair(pair, ahead):
    return follow(pair[:, :D], pair, ahead)


def chain_kernel(me_ref, *refs):
    pairs, move_ref, add_ref = refs[:-2], refs[-2], refs[-1]
    heads = move_ref.shape[0]
    for m in range(len(pairs)):

        @pl.when(me_ref[0] == m)
        def _():
            steps = [[pairs[m ^ b][h] for h in range(heads)] for b in range(len(pairs))]
            while len(steps) > 1:
                steps = [
                    [follow_pair(steps[b + 1][h], steps[b][h]) for h in range(heads)] for b in range(0, len(steps), 2)
                ]
            for h in range(heads):
                move_ref[h] = steps[0][h][:, :D]
                add_ref[h] = steps[0][h][:, D:]


def prefix_kernel(me_ref, *refs):
    pairs, before_ref = refs[:-1], refs[-1]
    heads = before_ref.shape[1]
    for m in range(len(pairs)):

        @pl.when(me_ref[0] == m)
        def _():
            now = [pairs[m][h] for h in range(heads)]
            for b in range(len(pairs) - 1):
                for h in range(heads):
                    if b:
                        now[h] = follow_pair(pairs[m ^ b][h], now[h])
                    before_ref[b, h] = now[h]


def absorb_kernel(count, wide, sends, which_ref, *refs):
    parts, refs = refs[:count], refs[count:]
    if sends:
        own_move, own_add, refs = refs[0], refs[1], refs[2:]
    have, outs = (refs[:2], refs[2:]) if wide else (None, refs)
    heads = parts[0].shape[0]
    for d in range(-1, count):

        @pl.when(which_ref[0] == d)
        def _():
            for h in range(heads):
                if d < 0:
                    ahead = have[1][h] if wide else jnp.zeros(parts[0].shape[1:], BF16)
                else:
                    ahead = follow(have[0][h], have[1][h], parts[d][h]) if wide else parts[d][h]
                outs[0][h] = ahead
                if sends:
                    outs[1][h] = follow(own_move[h], own_add[h], ahead)


def absorb_four_kernel(span_ref, move_ref, add_ref, came_ref, ahead_ref, state_ref, mixed_ref):
    for upper in (0, 1):

        @pl.when(span_ref[0] & 1 == upper)
        def _():
            for h in range(add_ref.shape[0]):
                ahead = came_ref[h] if upper else jnp.zeros(came_ref.shape[1:], BF16)
                state = follow(move_ref[h], add_ref[h], ahead) if upper else add_ref[h]
                ahead_ref[h] = ahead
                state_ref[h] = state
                mixed_ref[h] = state if upper else move_ref[h]


def starts_four_kernel(me_ref, span_ref, ahead_ref, near_ref, far_ref, before_ref, *outs):
    heads = ahead_ref.shape[0]

    def state_ahead(h):
        both = follow(near_ref[h], ahead_ref[h], far_ref[h])
        state = jnp.where(span_ref[0] == 3, both.astype(F32), ahead_ref[h].astype(F32))
        return jnp.where(span_ref[0] == 2, near_ref[h].astype(F32), state).astype(BF16)

    give_starts(me_ref, before_ref, [state_ahead(h) for h in range(heads)], outs)


def give_starts(me_ref, before_ref, first, outs):
    heads = len(first)
    later = [
        [follow(before_ref[b, h, :, :D], before_ref[b, h, :, D:], first[h]) for h in range(heads)]
        for b in range(len(outs) - 1)
    ]
    for m in range(len(outs)):

        @pl.when(me_ref[0] == m)
        def _():
            for b in range(len(outs)):
                for h in range(heads):
                    outs[m ^ b][h] = later[b - 1][h] if b else first[h]


def starts_kernel(count, me_ref, which_ref, *refs):
    parts, (move_ref, add_ref, before_ref, *outs) = refs[:count], refs[count:]
    heads = move_ref.shape[0]

    def state_ahead(h):
        came = jnp.zeros(move_ref.shape[1:], F32)
        for d in range(count):
            came = jnp.where(which_ref[0] == d, parts[d][h].astype(F32), came)
        return follow(move_ref[h], add_ref[h], came.astype(BF16))

    give_starts(me_ref, before_ref, [state_ahead(h) for h in range(heads)], outs)


def finish_kernel(count, more, *refs):
    groups, refs = refs[:count], refs[count:]
    refs = refs[1:] if more else refs
    reach, own, scale, starts = (refs[k * count : (k + 1) * count] for k in range(4))
    out_ref, held, sems = refs[4 * count :]
    heads = starts[0].shape[0]
    cols = heads * D
    copies = []
    for n in range(count):
        for h in range(heads):
            c = slice(h * D, (h + 1) * D)
            found = own[n][:, c] + dot(reach[n][:, c], starts[n][h])
            found = found.astype(BF16).astype(F32)
            mean = jnp.mean(found * found, -1, keepdims=True)
            held[n, :, c] = (found * lax.rsqrt(mean + 1e-5) * scale[n][:, c]).astype(BF16)
        to = pl.ds(pl.multiple_of(groups[n][0] * cols, cols), cols)
        copies.append(pltpu.make_async_copy(held.at[n], out_ref.at[:, to], sems.at[n]))
        copies[n].start()
    for copy in copies:
        copy.wait()


def whole_route(pairs, count):
    sources = [i for i in range(count) if i not in [a for a, _ in pairs]]
    targets = [i for i in range(count) if i not in [b for _, b in pairs]]
    if len(sources) <= 5:
        cost = lambda order: sum(abs(a - b) if a != b else count * count for a, b in zip(sources, order))
        targets = min(itertools.permutations(targets), key=cost)
    return pairs + list(zip(sources, targets))


def block_order(groups):
    if groups != 4:
        return [[j] for j in range(groups - 1, -1, -1)]
    return [[3], [1, 2, 0]]


def params():
    return pltpu.CompilerParams(vmem_limit_bytes=VMEM_LIMIT)


def shards(query_raw, key_raw, value_raw, log_decay, beta, conv_weight, out_gate, norm_gain):
    rows, width = query_raw.shape
    groups = lax.axis_size("head")
    spans = lax.axis_size("ctx")
    cols = width // groups
    heads = cols // D
    rim_width = conv_weight.shape[1] - 1
    me = lax.axis_index("head").astype(jnp.int32).reshape(1)
    span = lax.axis_index("ctx").astype(jnp.int32).reshape(1)
    group_ids = [me ^ j for j in range(groups)]
    later = (me + span > 0).astype(jnp.int32)
    rounds = (spans - 1).bit_length()
    places = [jnp.where((span >> r) & 1 > 0, span & ((1 << r) - 1), -1) for r in range(rounds)]
    (group_ids, later, places, span), query_raw, key_raw, value_raw, log_decay = lax.optimization_barrier(
        ((group_ids, later, places, span), query_raw, key_raw, value_raw, log_decay)
    )
    me_arg = group_ids[0]
    near = [pltpu.with_memory_space_constraint(x, pltpu.VMEM) for x in (key_raw, value_raw)]
    query_raw, key_raw, value_raw, log_decay, out_gate = (
        pltpu.with_memory_space_constraint(x, pltpu.HBM) for x in (query_raw, key_raw, value_raw, log_decay, out_gate)
    )
    beta = beta.T

    smem = pl.BlockSpec(memory_space=pltpu.SMEM)
    vmem = pl.BlockSpec(memory_space=pltpu.VMEM)
    far = pl.BlockSpec(memory_space=pl.ANY)

    tails = pl.pallas_call(
        functools.partial(tails_kernel, rim_width),
        in_specs=[far] * 3,
        out_specs=vmem,
        out_shape=jax.ShapeDtypeStruct((EDGE, width), BF16),
        scratch_shapes=[pltpu.VMEM((3, EDGE, width), BF16), pltpu.SemaphoreType.DMA((3,))],
        compiler_params=params(),
        name="tails",
    )(query_raw, key_raw, value_raw)
    total = groups * spans
    rim = lax.ppermute(tails, ("ctx", "head"), [(i, (i + 1) % total) for i in range(total)])

    wide16 = jax.ShapeDtypeStruct((rows, width), BF16)
    prepared = pl.pallas_call(
        functools.partial(prepare_kernel, groups),
        in_specs=[far] + [vmem] * 4,
        out_specs=[vmem] * 11,
        scratch_shapes=[pltpu.VMEM((rows, width), BF16), pltpu.SemaphoreType.DMA],
        out_shape=[wide16] * 6
        + [
            jax.ShapeDtypeStruct((rows, width), F32),
            jax.ShapeDtypeStruct((EDGE, width), F32),
            jax.ShapeDtypeStruct((8, width), F32),
            jax.ShapeDtypeStruct((2, EDGE, width), BF16),
            jax.ShapeDtypeStruct((EDGE, beta.shape[0]), F32),
        ],
        compiler_params=params(),
        cost_estimate=pl.CostEstimate(flops=20_000_000, bytes_accessed=9_000_000, transcendentals=2_000_000),
        name="prepare",
    )(log_decay, *near, beta, conv_weight)
    write, low, kin, khi, klo, vb, up, down, marks, edges, rates = prepared

    def call(kernel, name, in_specs, outs, scratch=()):
        return pl.pallas_call(
            kernel,
            in_specs=in_specs,
            out_specs=[vmem] * len(outs),
            out_shape=[jax.ShapeDtypeStruct(*out) for out in outs],
            scratch_shapes=scratch,
            compiler_params=params(),
            name=name,
        )

    def swap(array, j, axis="head"):
        return lax.ppermute(array, axis, [(i, i ^ j) for i in range(lax.axis_size(axis))])

    block16, block32 = ((rows, cols), BF16), ((rows, cols), F32)
    state, pair = ((heads, D, D), BF16), ((heads, D, 2 * D), BF16)

    def local(js):
        if not js:
            return {}
        got = call(
            functools.partial(local_kernel, len(js)),
            "local",
            [smem] * (1 + len(js)) + [vmem, far, far] + [vmem] * (4 + 2 * len(js)),
            [block16, block32, block32] * len(js),
            [pltpu.VMEM((2, len(js), rows, cols), BF16), pltpu.SemaphoreType.DMA((2, len(js)))],
        )(
            later, *[group_ids[j] for j in js], rim, query_raw, out_gate, conv_weight, norm_gain.reshape(1, D),
            up, marks, *[x for j in js for x in (lows[j], made[j])],
        )
        return {j: got[3 * i : 3 * i + 3] for i, j in enumerate(js)}

    moves, made, lows = ({} for _ in range(3))
    for js in block_order(groups):
        got = call(
            functools.partial(block_kernel, len(js)),
            "block",
            [smem] * (1 + len(js)) + [vmem] * 13,
            [pair, ((heads, rows, 2 * D), BF16), block16] * len(js),
        )(
            later, *[group_ids[j] for j in js], rim, edges, rates, conv_weight, up, down, marks, write, low, kin, khi,
            klo, vb,
        )
        for n, j in enumerate(js):
            moves[j], made[j], lows[j] = got[3 * n : 3 * n + 3]
    came_pairs = [swap(moves[j], j) if j else moves[j] for j in range(groups)]
    left = list(range(groups))
    came_pairs, found = lax.optimization_barrier((came_pairs, local(left[: groups // 2])))
    left = left[groups // 2 :]
    move, add = call(chain_kernel, "chain", [smem] + [vmem] * groups, [state] * 2)(me_arg, *came_pairs)

    def tell(array, r):
        half = 1 << r
        routes = [
            [(low + half - 1, low + half + d) for low in range(0, spans, 2 * half) if low + half + d < spans]
            for d in range(half)
        ]
        return [lax.ppermute(array, "ctx", whole_route(route, spans)) for route in routes if route]

    def absorb(r, parts, own, have):
        wide, sends = have is not None, own is not None
        return call(
            functools.partial(absorb_kernel, len(parts), wide, sends),
            "absorb",
            [smem] + [vmem] * (len(parts) + 2 * wide + 2 * sends),
            [state] * (1 + sends),
        )(places[r], *parts, *(own or ()), *(have or ()))

    adds = tell(add, 0) if rounds else []
    adds, mine = lax.optimization_barrier((adds, local(left)))
    found.update(mine)
    ahead, send_move = None, move
    if spans == 4:
        ahead, told, mixed = call(absorb_four_kernel, "absorb", [smem] + [vmem] * 3, [state] * 3)(
            span, move, add, adds[0]
        )
        adds = [
            lax.ppermute(mixed, "ctx", whole_route([(0, 1), (1, 2), (2, 3)], 4)),
            lax.ppermute(told, "ctx", [(1, 3), (3, 2), (2, 1), (0, 0)]),
        ]
    for r in range(rounds - 1 if spans != 4 else 0):
        moves_in = tell(send_move, r)
        got_add = absorb(r, adds, (move, add), ahead)
        adds = tell(got_add[1], r + 1)
        more = r + 2 < rounds
        got_move = absorb(r, moves_in, (move, move) if more else None, (ahead[0], ahead[0]) if ahead else None)
        ahead = (got_move[0], got_add[0])
        send_move = got_move[1] if more else None
    (before,) = call(
        prefix_kernel, "prefix", [smem] + [vmem] * groups, [((groups - 1, heads, D, 2 * D), BF16)]
    )(me_arg, *came_pairs)
    adds, before = lax.optimization_barrier((adds, before))
    if spans == 4:
        starts = call(starts_four_kernel, "starts", [smem] * 2 + [vmem] * 4, [state] * groups)(
            me_arg, span, ahead, *adds, before
        )
    else:
        ahead = (jnp.zeros(*state),) * 2 if ahead is None else ahead
        starts = call(
            functools.partial(starts_kernel, len(adds)),
            "starts",
            [smem] * 2 + [vmem] * (len(adds) + 3),
            [state] * groups,
        )(me_arg, places[-1] if rounds else later, *adds, *ahead, before)
    starts = [starts[0]] + [swap(starts[j], j) for j in range(1, groups)]

    def finish(js, out):
        more = out is not None
        return pl.pallas_call(
            functools.partial(finish_kernel, len(js), more),
            in_specs=[smem] * len(js) + [far] * more + [vmem] * (4 * len(js)),
            out_specs=far,
            out_shape=jax.ShapeDtypeStruct((rows, width), BF16),
            scratch_shapes=[pltpu.VMEM((len(js), rows, cols), BF16), pltpu.SemaphoreType.DMA((len(js),))],
            input_output_aliases={len(js): 0} if more else {},
            compiler_params=params(),
            name="finish",
        )(
            *[group_ids[j] for j in js], *([out] if more else []),
            *[found[j][k] for k in range(3) for j in js], *[starts[j] for j in js],
        )

    first = [j for j in (0, FIRST) if j < groups]
    rest = [j for j in range(groups) if j not in first]
    out = finish(first, None)
    return finish(rest, out) if rest else out


def solution(mesh):
    tokens = P(("dp", "ctx", "head"), None)
    placed = (tokens, tokens, tokens, tokens, tokens, P(), tokens, P())
    return jax.shard_map(shards, mesh=mesh, in_specs=placed, out_specs=tokens, check_vma=False)
```
